512 devices in a mesh: group: 16 (over x_lo, z), tile: 32 (over x_hi, y, core).
Axes of the slice: x: 4 (x_hi: 2, x_lo: 2; x = x_hi * 2 + x_lo), y: 8, z: 8, core: 2. Of those that a mesh axis runs over, the one named last changes fastest.
Arguments:
- initial_state: float32 [48, 2, 128, 384], P(None, None, 'tile'), may hold values from -3 to 3
- perturbation: float32 [16, 48, 2, 128, 384], P('group', None, None, 'tile'), may hold values from -16 to 16
- land_sea: int32 [128, 384], P('tile'), may hold values 0 or 1
- relax_level: int32 [128, 384], P('tile'), may hold values from 0 to 3
- vertical_mix: float32 [48], replicated, may hold values from 0.1 to 2
Outputs:
- adjoint_field: float32 [16, 48, 2, 128, 384], P('group', None, None, 'tile')
- gram: float32 [16, 16], P('group')
The draws below stay inside these ranges and needn't reach their ends.
All inputs are finite; a program needn't handle non-finite values. No bound on the sum of `land_sea` on one device may be relied on, other than what follows from the above.
Results may differ from the reference program's by a relative error of at most 0.00024.
Values sent between devices are 32-bit elements; how exact they have to be, the bound alone decides.
No kernel may reach another device: no remote copies, remote signals or barrier semaphores. Data moves between devices by JAX's collectives and lax.ppermute only.
A program may use at most 64 MiB of HBM per device.

```python
import math
import jax
import jax.numpy as jnp
from jax import lax

FIELDS = 2
LEV = 48
NY = 384
STEPS = 3
NX = 128
MEMBERS = 16


def draw_perturbation(key, part):
    dims_all = (MEMBERS, LEV, FIELDS, NX, NY)
    x_ramp = 1.0 + 2.0 * jnp.arange(NX, dtype=jnp.float32) / (NX - 1)
    values = jax.random.normal(key, dims_all, jnp.float32)
    values = values * x_ramp[None, None, None, :, None]
    return jnp.clip(values, -16.0, 16.0)


def with_ends(entries, rng, least, top_value):
    longest = entries.shape.index(max(entries.shape))
    spots = []
    for shift in (0, 1):
        where = [jax.random.randint(jax.random.fold_in(rng, axis), (), 0, length) for axis, length in enumerate(entries.shape)]
        where[longest] = (where[longest] + shift) % entries.shape[longest]
        spots.append(tuple(where))
    return entries.at[spots[0]].set(least).at[spots[1]].set(top_value)


def levels(key, shape, split, least, largest):
    level = 1.0
    for dim, blocks in split:
        heights = jax.random.uniform(jax.random.fold_in(jax.random.fold_in(key, 6), dim), (blocks,), jnp.float32, least / len(split), largest / len(split))
        level = level * jnp.repeat(jnp.exp(heights), shape[dim] // blocks).reshape((-1,) + (1,) * (len(shape) - 1 - dim))
    return level


def normal_values(own_key, dims, spread, reach, cuts=(), held_as=jnp.bfloat16):
    result = jax.random.normal(own_key, dims, jnp.float32) * spread
    if len(cuts) > 0:
        result = levels(own_key, dims, cuts, -0.22, 0.18) * result
    return jnp.clip(result, min=-reach, max=reach).astype(held_as)


def setup_inputs(seed: int = 0) -> dict:
    seeds = jax.random.split(jax.random.key(seed), 6)
    return {
        "initial_state": normal_values(seeds[0], (LEV, FIELDS, NX, NY), 0.8, 3.0, ((2, 32),), jnp.float32),
        "perturbation": draw_perturbation(jax.random.fold_in(seeds[5], 71), 0),
        "land_sea": with_ends((jax.random.randint(seeds[2], (NX, NY), 0, 5) < 2).astype(jnp.int32), jax.random.fold_in(seeds[2], 1), 0, 1),
        "relax_level": with_ends(jax.random.randint(seeds[3], (NX, NY), 0, 4), jax.random.fold_in(seeds[3], 1), 0, 3).astype(jnp.int32),
        "vertical_mix": jnp.clip(jnp.exp(jax.random.uniform(seeds[4], (LEV,), jnp.float32, math.log(0.1), math.log(2.0))), 0.1, 2.0),
    }


advection = 0.2
diffusion = 0.1
drag_rate = 0.3
relaxation = 0.125

def row_slope(padded):
    return 0.5 * (padded[:, :, 2:] - padded[:, :, :-2])

def laplace(padded):
    centre = padded[:, :, 1:-1]
    widened = jnp.pad(centre, ((0, 0), (0, 0), (0, 0), (1, 1)))
    return padded[:, :, 2:] + padded[:, :, :-2] + widened[..., 2:] + widened[..., :-2] - 4.0 * centre

def pad_rows(field):
    return jnp.pad(field, ((0, 0), (0, 0), (1, 1), (0, 0)))

def column_solve(columns, mixing):
    layout = columns.shape
    nothing = jnp.zeros((1,), jnp.float32)
    upper_band = jnp.concatenate([-mixing[:-1], nothing])
    lower_band = jnp.concatenate([nothing, -mixing[:-1]])
    diagonal_band = 1.0 + mixing + jnp.concatenate([nothing, mixing[:-1]])
    solved = lax.linalg.tridiagonal_solve(lower_band, diagonal_band, upper_band, columns.reshape(layout[0], -1))
    return solved.reshape(layout)

def reference(initial_state, perturbation, land_sea, relax_level, vertical_mix):
    landmask = land_sea.astype(jnp.float32)
    nudging = 1.0 - relaxation * relax_level.astype(jnp.float32)
    select = (jnp.arange(2) == 0).astype(jnp.float32)[None, :, None, None]
    current = initial_state
    history = []
    for position in range(STEPS):
        padded = pad_rows(current)
        slopes = row_slope(padded)
        zonal_wind = current[:, 0:1]
        history.append((zonal_wind, slopes))
        if position + 1 < STEPS:
            updated = current - advection * zonal_wind * slopes + diffusion * laplace(padded) - drag_rate * landmask * select * current
            current = column_solve(updated * nudging, vertical_mix)

    def forward(tangent):
        for zonal_wind, slopes in history:
            tangent_pad = pad_rows(tangent)
            updated = tangent - advection * (tangent[:, 0:1] * slopes + zonal_wind * row_slope(tangent_pad)) + diffusion * laplace(tangent_pad) - drag_rate * landmask * select * tangent
            tangent = column_solve(updated * nudging, vertical_mix)
        return tangent

    def member_run(member):
        forward_out, pullback = jax.vjp(forward, member)
        return pullback(forward_out)[0]
    adjoint_field = lax.map(member_run, perturbation)
    flattened = adjoint_field.reshape(adjoint_field.shape[0], -1)
    gram = jnp.dot(flattened, flattened.T, precision=lax.Precision.HIGHEST) / flattened.shape[1]
    return (adjoint_field, gram)
```

```python
import functools

import jax
import jax.numpy as jnp
from jax import lax
from jax.experimental import pallas as pl
from jax.experimental.pallas import tpu as pltpu
from jax.sharding import PartitionSpec as P

advection = 0.2
diffusion = 0.1
drag_rate = 0.3
relaxation = 0.125

VMEM_LIMIT = 24 * 2**20

ANY = pl.BlockSpec(memory_space=pl.ANY)
VMEM = pl.BlockSpec(memory_space=pltpu.VMEM)
SMEM = pl.BlockSpec(memory_space=pltpu.SMEM)


def run(kernel, out_shape, in_specs, out_specs, scratch, flops=0, nbytes=0):
    return pl.pallas_call(
        kernel,
        out_shape=out_shape,
        in_specs=in_specs,
        out_specs=out_specs,
        scratch_shapes=scratch,
        compiler_params=pltpu.CompilerParams(vmem_limit_bytes=VMEM_LIMIT),
        cost_estimate=pl.CostEstimate(flops=flops, bytes_accessed=nbytes, transcendentals=0),
    )


def f32(*shape):
    return jax.ShapeDtypeStruct(shape, jnp.float32)


def start_all(copies):
    for copy in copies:
        copy.start()


def wait_all(copies):
    for copy in copies:
        copy.wait()


def pack_rows(src, dst, sems):
    lev, fields, rows, _ = src.shape
    return [
        pltpu.make_async_copy(
            src.at[:, f, r, :], dst.at[pl.ds((f * rows + r) * lev, lev), :], sems.at[f * rows + r]
        )
        for f in range(fields)
        for r in range(rows)
    ]


def pack_state_kernel(x, land, relax, out, sems):
    copies = pack_rows(x, out, sems)
    start_all(copies)
    rows = land.shape[0]
    end = out.shape[0] - 2 * rows
    out[end : end + rows, :] = 1.0 - relaxation * relax[...].astype(jnp.float32)
    out[end + rows :, :] = drag_rate * land[...].astype(jnp.float32)
    wait_all(copies)


def pack_field_kernel(x, out, sems):
    copies = pack_rows(x, out, sems)
    start_all(copies)
    wait_all(copies)


def inverse_kernel(mix, once, twice, solved):
    lev = mix.shape[0]
    wide = solved.shape[1]
    lane = lax.broadcasted_iota(jnp.int32, (1, wide), 1)
    unit = lane % lev
    ratio = []
    before = None
    inv = None
    for l in range(lev):
        rhs = jnp.where(unit == l, 1.0, 0.0).astype(jnp.float32)
        if l == 0:
            diag = jnp.full((1, wide), 1.0 + mix[0], jnp.float32)
        else:
            m = mix[l - 1]
            diag = (1.0 + mix[l] + m) - (m * m) * inv
            rhs = rhs + m * before
        inv = 1.0 / diag
        before = rhs * inv
        solved[l : l + 1, :] = before
        ratio.append(inv)
    for l in reversed(range(lev - 1)):
        before = solved[l : l + 1, :] + mix[l] * ratio[l] * before
        solved[l : l + 1, :] = before
    single = solved[...]
    double = jnp.dot(
        single[:, :lev],
        single,
        precision=lax.Precision.HIGHEST,
        preferred_element_type=jnp.float32,
    )
    third = lax.broadcasted_iota(jnp.int32, (lev, wide), 1) >= 2 * lev
    for matrix, out in ((single, once), (double, twice)):
        head = matrix.astype(jnp.bfloat16)
        tail = matrix - head.astype(jnp.float32)
        out[...] = jnp.where(third, tail, head.astype(jnp.float32)).astype(jnp.bfloat16)


def read(buf, base, f, i, lev):
    return buf[f, pl.ds(pl.multiple_of((i - base) * lev, 8), lev), :]


def write(buf, base, f, i, lev, value):
    buf[f, pl.ds(pl.multiple_of((i - base) * lev, 8), lev), :] = value


def tiled(block, lev):
    return jnp.concatenate([block] * (lev // 8), axis=0)


def solve(matrix, first, second):
    both = jnp.concatenate([first, second], axis=1)
    head = both.astype(jnp.bfloat16)
    tail = (both - head.astype(jnp.float32)).astype(jnp.bfloat16)
    out = jnp.dot(
        matrix, jnp.concatenate([head, tail, head], axis=0), preferred_element_type=jnp.float32
    )
    half = first.shape[1]
    return out[:, :half], out[:, half:]


def beside(value, lane):
    width = value.shape[1]
    east = jnp.where(lane < width - 1, pltpu.roll(value, width - 1, 1), 0.0)
    west = jnp.where(lane > 0, pltpu.roll(value, 1, 1), 0.0)
    return east + west


def fill_factors(borders, factors):
    for j in range(3):
        for r in range(4):
            for kind in range(2):
                line = borders[j, pl.ds(4 * kind + r, 1), :]
                factors[4 * j + r, kind] = jnp.broadcast_to(line, factors.shape[2:])


def row_loop(first, last, body):
    def pair(k, carry):
        body(first + 2 * k)
        body(first + 2 * k + 1)
        return carry

    lax.fori_loop(0, (last - first) // 2, pair, 0)


def state_row(i, x, xbase, factors, matrix, out, obase, lev):
    keep, drag = factors[i + 4, 0], factors[i + 4, 1]
    near = tiled(diffusion * keep, lev)
    wind = read(x, xbase, 0, i, lev)
    lane = lax.broadcasted_iota(jnp.int32, wind.shape, 1)
    parts = []
    for f in range(2):
        centre = wind if f == 0 else read(x, xbase, f, i, lev)
        up = read(x, xbase, f, i + 1, lev)
        down = read(x, xbase, f, i - 1, lev)
        own = tiled(keep * (0.6 - drag) if f == 0 else 0.6 * keep, lev)
        around = (up + down) + beside(centre, lane) - wind * (up - down)
        parts.append(own * centre + near * around)
    for f, value in enumerate(solve(matrix, *parts)):
        write(out, obase, f, i, lev, value)


def tangent_row(i, d, dbase, x, xbase, factors, matrix, out, obase, lev, damp):
    keep, drag = factors[i + 4, 0], factors[i + 4, 1]
    near = tiled(diffusion * keep, lev)
    wind = read(x, xbase, 0, i, lev)
    du = read(d, dbase, 0, i, lev)
    lane = lax.broadcasted_iota(jnp.int32, wind.shape, 1)
    parts = []
    for f in range(2):
        centre = du if f == 0 else read(d, dbase, f, i, lev)
        up = read(d, dbase, f, i + 1, lev)
        down = read(d, dbase, f, i - 1, lev)
        slope = read(x, xbase, f, i + 1, lev) - read(x, xbase, f, i - 1, lev)
        own = tiled(keep * (0.6 - drag) if f == 0 else 0.6 * keep, lev)
        around = (up + down) + beside(centre, lane) - wind * (up - down) - du * slope
        parts.append(own * centre + near * around)
    for f, value in enumerate(solve(matrix, *parts)):
        write(out, obase, f, i, lev, value * tiled(keep, lev) if damp else value)


def adjoint_row(i, b, bbase, x, xbase, factors, lev):
    drag = factors[i + 4, 1]
    lane = lax.broadcasted_iota(jnp.int32, (lev, b.shape[2]), 1)
    more = 1.0 + read(x, xbase, 0, i + 1, lev)
    less = 1.0 - read(x, xbase, 0, i - 1, lev)
    parts = []
    sloped = 0.0
    for f in range(2):
        centre = read(b, bbase, f, i, lev)
        up = read(b, bbase, f, i + 1, lev)
        down = read(b, bbase, f, i - 1, lev)
        sloped = sloped + centre * (read(x, xbase, f, i + 1, lev) - read(x, xbase, f, i - 1, lev))
        around = more * up + less * down + beside(centre, lane)
        parts.append((centre, around))
    wind_part = tiled(0.6 - drag, lev) * parts[0][0] + diffusion * (parts[0][1] - sloped)
    heat_part = 0.6 * parts[1][0] + diffusion * parts[1][1]
    return wind_part, heat_part


def border_copies(own, left, right, buf, borders, sems, first, last, rows, lev):
    copies = []
    for j, src in enumerate((left, own, right)):
        low = max(first - rows * (j - 1), 0)
        high = min(last - rows * (j - 1), rows)
        for f in range(2):
            copies.append(
                pltpu.make_async_copy(
                    src.at[pl.ds((f * rows + low) * lev, (high - low) * lev), :],
                    buf.at[f, pl.ds((low + rows * (j - 1) - first) * lev, (high - low) * lev), :],
                    sems.at[3 * f + j],
                )
            )
        if borders is not None:
            copies.append(
                pltpu.make_async_copy(
                    src.at[pl.ds(2 * rows * lev, 2 * rows), :], borders.at[j], sems.at[6 + j]
                )
            )
    return copies


def trajectory_kernel(own, left, right, once, x1, x2, x0, borders, factors, sems, *, lev):
    copies = border_copies(own, left, right, x0, borders, sems, -4, 8, 4, lev)
    start_all(copies)
    wait_all(copies)
    fill_factors(borders, factors)
    matrix = once[...]
    row_loop(-3, 7, lambda i: state_row(i, x0, -4, factors, matrix, x1, -3, lev))
    row_loop(-2, 6, lambda i: state_row(i, x1, -3, factors, matrix, x2, -2, lev))


def forward_kernel(
    own, left, right, p_own, p_left, p_right, x1, x2, once, twice,
    low_rows, high_rows,
    x0, borders, factors, p, t1, t2, b2, x_sems, p_sems, *, lev,
):
    copies = border_copies(p_own, p_left, p_right, p, None, p_sems, -4, 8, 4, lev)
    copies += border_copies(own, left, right, x0, borders, x_sems, -4, 8, 4, lev)
    start_all(copies)
    wait_all(copies)
    fill_factors(borders, factors)
    matrix = once[...]
    square = twice[...]
    row_loop(
        -3, 7, lambda i: tangent_row(i, p, -4, x0, -4, factors, matrix, t1, -3, lev, False)
    )
    row_loop(
        -2, 6, lambda i: tangent_row(i, t1, -3, x1, -3, factors, matrix, t2, -2, lev, False)
    )
    row_loop(
        -1, 5, lambda i: tangent_row(i, t2, -2, x2, -2, factors, square, b2, -1, lev, True)
    )

    def last(out, obase, i):
        keep = tiled(factors[i + 4, 0], lev)
        parts = adjoint_row(i, b2, -1, x2, -2, factors, lev)
        for f, value in enumerate(solve(matrix, *parts)):
            write(out, obase, f, i, lev, value * keep)

    row_loop(0, 2, lambda i: last(low_rows, 0, i))
    row_loop(2, 4, lambda i: last(high_rows, 2, i))


def backward_kernel(
    own, left, right, x1, b_left, b_low, b_high, b_right, once,
    packed, field,
    x0, borders, factors, b1, b0, x_sems, b_sems, out_sems, *, lev,
):
    copies = [
        pltpu.make_async_copy(
            src, b1.at[:, pl.ds(2 * lev * k, 2 * lev), :], b_sems.at[k]
        )
        for k, src in enumerate((b_left, b_low, b_high, b_right))
    ]
    copies += border_copies(own, left, right, x0, borders, x_sems, -1, 5, 4, lev)
    start_all(copies)
    wait_all(copies)
    fill_factors(borders, factors)
    matrix = once[...]

    def middle(i):
        keep = tiled(factors[i + 4, 0], lev)
        parts = adjoint_row(i, b1, -2, x1, -3, factors, lev)
        for f, value in enumerate(solve(matrix, *parts)):
            write(b0, -1, f, i, lev, value * keep)

    row_loop(-1, 5, middle)

    outs = []
    for i in range(4):
        parts = adjoint_row(i, b0, -1, x0, -1, factors, lev)
        for f, value in enumerate(parts):
            k = 4 * f + i
            packed[k * lev : (k + 1) * lev, :] = value
            copy = pltpu.make_async_copy(
                packed.at[pl.ds(k * lev, lev), :], field.at[:, f, i, :], out_sems.at[k]
            )
            copy.start()
            outs.append(copy)
    wait_all(outs)


def per_device(initial_state, perturbation, land_sea, relax_level, vertical_mix):
    lev, fields, rows, width = initial_state.shape
    tiles = lax.axis_size("tile")
    members = lax.axis_size("group")
    high = fields * rows * lev
    dma = pltpu.SemaphoreType.DMA
    rightward = [(i, i + 1) for i in range(tiles - 1)]
    leftward = [(i + 1, i) for i in range(tiles - 1)]

    def from_left(value):
        return lax.ppermute(value, "tile", rightward)

    def from_right(value):
        return lax.ppermute(value, "tile", leftward)

    def buffer(n):
        return pltpu.VMEM((fields, n * lev, width), jnp.float32)

    state = run(
        pack_state_kernel,
        f32(high + 2 * rows, width),
        [ANY, VMEM, VMEM],
        VMEM,
        [dma((fields * rows,))],
        nbytes=2**20,
    )(initial_state, land_sea, relax_level)
    state_left, state_right = from_left(state), from_right(state)
    start = run(
        pack_field_kernel, f32(high, width), [ANY], VMEM, [dma((fields * rows,))], nbytes=2**20
    )(perturbation[0])
    start_left, start_right = from_left(start), from_right(start)

    weights = jax.ShapeDtypeStruct((lev, 3 * lev), jnp.bfloat16)
    once, twice = run(
        inverse_kernel,
        (weights, weights),
        [SMEM],
        (VMEM, VMEM),
        [pltpu.VMEM((lev, 3 * lev), jnp.float32)],
        nbytes=2**20,
    )(vertical_mix)

    borders = pltpu.VMEM((3, 2 * rows, width), jnp.float32)
    factors = pltpu.VMEM((3 * rows, 2, 8, width), jnp.float32)
    x1, x2 = run(
        functools.partial(trajectory_kernel, lev=lev),
        (f32(fields, 10 * lev, width), f32(fields, 8 * lev, width)),
        [ANY, ANY, ANY, VMEM],
        (VMEM, VMEM),
        [buffer(12), borders, factors, dma((9,))],
        nbytes=6 * 2**20,
    )(state, state_left, state_right, once)

    low_rows, high_rows = run(
        functools.partial(forward_kernel, lev=lev),
        (f32(fields, 2 * lev, width), f32(fields, 2 * lev, width)),
        [ANY] * 6 + [VMEM] * 4,
        (VMEM, VMEM),
        [buffer(12), borders, factors, buffer(12), buffer(10), buffer(8), buffer(6)]
        + [dma((9,)), dma((6,))],
        nbytes=10 * 2**20,
    )(state, state_left, state_right, start, start_left, start_right, x1, x2, once, twice)

    b_left, b_right = from_left(high_rows), from_right(low_rows)
    packed, field = run(
        functools.partial(backward_kernel, lev=lev),
        (f32(high, width), f32(lev, fields, rows, width)),
        [ANY, ANY, ANY, VMEM, ANY, ANY, ANY, ANY, VMEM],
        (VMEM, ANY),
        [buffer(6), borders, factors, buffer(8), buffer(6)]
        + [dma((9,)), dma((4,)), dma((fields * rows,))],
        nbytes=6 * 2**20,
    )(state, state_left, state_right, x1, b_left, low_rows, high_rows, b_right, once)

    share = lax.all_to_all(
        packed.reshape(members, high // members, width), "group", 0, 0, tiled=True
    )
    products = lax.dot_general(
        share,
        share,
        (((1, 2), (1, 2)), ((), ())),
        precision=lax.Precision.HIGHEST,
        preferred_element_type=jnp.float32,
    )
    row = jnp.sum(lax.all_to_all(products, "group", 0, 0, tiled=True), axis=0)
    spread = jnp.broadcast_to(row[None], (tiles, members))
    row = jnp.sum(lax.all_to_all(spread, "tile", 0, 0, tiled=True), axis=0)
    gram = row[None] / (high * width * tiles)
    return (field[None], gram)


def solution(mesh):
    placed = (
        P(None, None, "tile", None),
        P("group", None, None, "tile", None),
        P("tile", None),
        P("tile", None),
        P(),
    )
    return jax.shard_map(
        per_device,
        mesh=mesh,
        in_specs=placed,
        out_specs=(P("group", None, None, "tile", None), P("group", None)),
        check_vma=False,
    )
```

```python
import jax
import jax.numpy as jnp
from jax import lax
from jax.experimental import pallas as pl
from jax.experimental.pallas import tpu as pltpu
from jax.sharding import PartitionSpec as P

advection = 0.2
diffusion = 0.1
drag_rate = 0.3
relaxation = 0.125

VMEM_LIMIT = 24 * 2**20

ANY = pl.BlockSpec(memory_space=pl.ANY)
VMEM = pl.BlockSpec(memory_space=pltpu.VMEM)
SMEM = pl.BlockSpec(memory_space=pltpu.SMEM)


def run(kernel, out_shape, in_specs, out_specs, scratch, nbytes, limit=VMEM_LIMIT):
    return pl.pallas_call(
        kernel,
        out_shape=out_shape,
        in_specs=in_specs,
        out_specs=out_specs,
        scratch_shapes=scratch,
        compiler_params=pltpu.CompilerParams(vmem_limit_bytes=limit),
        cost_estimate=pl.CostEstimate(flops=0, bytes_accessed=nbytes, transcendentals=0),
    )


def f32(*shape):
    return jax.ShapeDtypeStruct(shape, jnp.float32)


def start_all(copies):
    for copy in copies:
        copy.start()


def wait_all(copies):
    for copy in copies:
        copy.wait()


def pack_rows(src, dst, sems, flipped):
    lev, fields, rows, _ = src.shape
    copies = []
    for f in range(fields):
        for r in range(rows):
            place = f * rows + jnp.where(flipped, rows - 1 - r, r)
            copies.append(
                pltpu.make_async_copy(
                    src.at[:, f, r, :],
                    dst.at[pl.ds(pl.multiple_of(place * lev, 8), lev), :],
                    sems.at[f * rows + r],
                )
            )
    return copies


def fill_lines(ints, out, flipped):
    rows = ints.shape[1]
    end = out.shape[0] - 2 * rows
    keep = 1.0 - relaxation * ints[0].astype(jnp.float32)
    drag = drag_rate * ints[1].astype(jnp.float32)
    for k, values in enumerate((keep, drag)):
        for r in range(rows):
            other = rows - 1 - r
            line = jnp.where(flipped, values[other : other + 1], values[r : r + 1])
            out[end + k * rows + r : end + k * rows + r + 1, :] = line


def pack_state_kernel(side, x, land, relax, out, sems, ints, more_sems, staged, out_sems):
    flipped = side[0] < 0.0
    loads = [
        pltpu.make_async_copy(src, ints.at[k], more_sems.at[k])
        for k, src in enumerate((relax, land))
    ]
    copies = pack_rows(x, staged, sems, flipped)
    start_all(loads)
    start_all(copies)
    wait_all(loads)
    fill_lines(ints, staged, flipped)
    lev, fields, rows, _ = x.shape
    places = [
        (f * rows + jnp.where(flipped, rows - 1 - r, r)) * lev
        for f in range(fields)
        for r in range(rows)
    ]
    pieces = [pl.ds(pl.multiple_of(place, 8), lev) for place in places]
    pieces.append(pl.ds(fields * rows * lev, 2 * rows))
    outs = [
        pltpu.make_async_copy(staged.at[piece], out.at[piece], out_sems.at[k])
        for k, piece in enumerate(pieces)
    ]
    outs[-1].start()
    for copy, onward in zip(copies, outs):
        copy.wait()
        onward.start()
    wait_all(outs)


def pack_field_kernel(side, x, out, sems):
    copies = pack_rows(x, out, sems, side[0] < 0.0)
    start_all(copies)
    wait_all(copies)


def inverse_kernel(mix, once, twice, solved):
    lev = mix.shape[0]
    wide = solved.shape[1]
    lane = lax.broadcasted_iota(jnp.int32, (1, wide), 1)
    unit = lane % lev
    ratio = []
    before = None
    inv = None
    for l in range(lev):
        rhs = jnp.where(unit == l, 1.0, 0.0).astype(jnp.float32)
        if l == 0:
            diag = jnp.full((1, wide), 1.0 + mix[0], jnp.float32)
        else:
            m = mix[l - 1]
            diag = (1.0 + mix[l] + m) - (m * m) * inv
            rhs = rhs + m * before
        inv = 1.0 / diag
        before = rhs * inv
        solved[l : l + 1, :] = before
        ratio.append(inv)
    for l in reversed(range(lev - 1)):
        before = solved[l : l + 1, :] + mix[l] * ratio[l] * before
        solved[l : l + 1, :] = before
    single = solved[...]
    double = jnp.dot(
        single[:, :lev],
        single,
        precision=lax.Precision.HIGHEST,
        preferred_element_type=jnp.float32,
    )
    third = lax.broadcasted_iota(jnp.int32, (lev, wide), 1) >= 2 * lev
    for matrix, out in ((single, once), (double, twice)):
        head = matrix.astype(jnp.bfloat16)
        tail = matrix - head.astype(jnp.float32)
        out[...] = jnp.where(third, tail, head.astype(jnp.float32)).astype(jnp.bfloat16)


class Rows:
    def __init__(self, lev, *pieces):
        self.lev = lev
        self.where = {}
        for buf, rows in pieces:
            for k, i in enumerate(rows):
                for f in range(2):
                    self.where[f, i] = (buf, (f * len(rows) + k) * lev)

    def read(self, f, i):
        buf, at = self.where[f, i]
        return buf[at : at + self.lev, :]

    def write(self, f, i, value):
        buf, at = self.where[f, i]
        buf[at : at + self.lev, :] = value


OWN = (0, 1, 2, 3)
OUTER = (-1, -2, -3, -4)
INNER = (7, 6, 5, 4)


def state_rows(own, outer, inner):
    lev = (own.shape[0] - 8) // 8
    return Rows(lev, (own, OWN), (outer, OUTER), (inner, INNER))


class Factors:
    def __init__(self, own, outer, inner):
        self.end = own.shape[0] - 8
        self.lev = self.end // 8
        self.where = {}
        for buf, rows in ((own, OWN), (outer, OUTER), (inner, INNER)):
            for k, i in enumerate(rows):
                self.where[i] = (buf, k)

    def line(self, i, kind):
        buf, k = self.where[i]
        at = self.end + 4 * kind + k
        return jnp.broadcast_to(buf[at : at + 1, :], (8, buf.shape[1]))

    def keep(self, i):
        return self.line(i, 0)

    def drag(self, i):
        return self.line(i, 1)


def tiled(block, lev):
    return jnp.concatenate([block] * (lev // 8), axis=0)


def solve(matrix, first, second):
    both = jnp.concatenate([first, second], axis=1)
    head = both.astype(jnp.bfloat16)
    tail = (both - head.astype(jnp.float32)).astype(jnp.bfloat16)
    out = jnp.dot(
        matrix, jnp.concatenate([head, tail, head], axis=0), preferred_element_type=jnp.float32
    )
    half = first.shape[1]
    return out[:, :half], out[:, half:]


def beside(value):
    lev, width = value.shape
    step = 128
    lane = lax.broadcasted_iota(jnp.int32, (lev, step), 1)
    parts = [value[:, c : c + step] for c in range(0, width, step)]
    up = [pltpu.roll(part, 1, 1) for part in parts]
    down = [pltpu.roll(part, step - 1, 1) for part in parts]
    zero = jnp.zeros_like(up[0])
    sums = []
    for k in range(len(parts)):
        west = jnp.where(lane == 0, up[k - 1] if k > 0 else zero, up[k])
        east = jnp.where(lane == step - 1, down[k + 1] if k + 1 < len(parts) else zero, down[k])
        sums.append(west + east)
    return jnp.concatenate(sums, axis=1)


def state_row(i, side, x, factors, matrix, out):
    lev = x.lev
    keep, drag = factors.keep(i), factors.drag(i)
    near = tiled(diffusion * keep, lev)
    wind = side * x.read(0, i)
    parts = []
    for f in range(2):
        centre = x.read(f, i)
        up, down = x.read(f, i + 1), x.read(f, i - 1)
        own = tiled(keep * (0.6 - drag) if f == 0 else 0.6 * keep, lev)
        around = (up + down) + beside(centre) - wind * (up - down)
        parts.append(own * centre + near * around)
    for f, value in enumerate(solve(matrix, *parts)):
        out.write(f, i, value)


def tangent_row(i, side, d, x, factors, matrix, out, damp):
    lev = x.lev
    keep, drag = factors.keep(i), factors.drag(i)
    near = tiled(diffusion * keep, lev)
    wind = side * x.read(0, i)
    du = side * d.read(0, i)
    parts = []
    for f in range(2):
        centre = d.read(f, i)
        up, down = d.read(f, i + 1), d.read(f, i - 1)
        slope = x.read(f, i + 1) - x.read(f, i - 1)
        own = tiled(keep * (0.6 - drag) if f == 0 else 0.6 * keep, lev)
        around = (up + down) + beside(centre) - wind * (up - down) - du * slope
        parts.append(own * centre + near * around)
    for f, value in enumerate(solve(matrix, *parts)):
        out.write(f, i, value * tiled(keep, lev) if damp else value)


def adjoint_row(i, side, b, x, factors):
    lev = x.lev
    drag = factors.drag(i)
    more = 1.0 + side * x.read(0, i + 1)
    less = 1.0 - side * x.read(0, i - 1)
    parts = []
    sloped = 0.0
    for f in range(2):
        centre = b.read(f, i)
        sloped = sloped + centre * (x.read(f, i + 1) - x.read(f, i - 1))
        around = more * b.read(f, i + 1) + less * b.read(f, i - 1) + beside(centre)
        parts.append((centre, around))
    wind_part = tiled(0.6 - drag, lev) * parts[0][0] + diffusion * (parts[0][1] - side * sloped)
    heat_part = 0.6 * parts[1][0] + diffusion * parts[1][1]
    return wind_part, heat_part


def adjoint_solved(i, side, b, x, factors, matrix, out):
    keep = tiled(factors.keep(i), x.lev)
    for f, value in enumerate(solve(matrix, *adjoint_row(i, side, b, x, factors))):
        out.write(f, i, value * keep)


def span(first, last):
    return tuple(range(first, last))


def trajectory_kernel(side, own, inner, outer, once, x1, x2):
    sign = side[0]
    first = state_rows(own, outer, inner)
    factors = Factors(own, outer, inner)
    lev = first.lev
    second = Rows(lev, (x1, span(-3, 7)))
    third = Rows(lev, (x2, span(-2, 6)))
    for i in span(-3, 7):
        state_row(i, sign, first, factors, once[...], second)
    for i in span(-2, 6):
        state_row(i, sign, second, factors, once[...], third)


def forward_kernel(
    side, own, inner, outer, p_own, p_inner, p_outer, x1, x2, once, twice,
    outer_rows, inner_rows,
    t1, t2, b2,
):
    sign = side[0]
    first = state_rows(own, outer, inner)
    factors = Factors(own, outer, inner)
    lev = first.lev
    second = Rows(lev, (x1, span(-3, 7)))
    third = Rows(lev, (x2, span(-2, 6)))
    start = Rows(lev, (p_own, OWN), (p_outer, OUTER), (p_inner, INNER))
    once_moved = Rows(lev, (t1, span(-3, 7)))
    twice_moved = Rows(lev, (t2, span(-2, 6)))
    back = Rows(lev, (b2, span(-1, 5)))
    out = Rows(lev, (outer_rows, (0, 1)), (inner_rows, (3, 2)))
    for i in span(-3, 7):
        tangent_row(i, sign, start, first, factors, once[...], once_moved, False)
    for i in span(-2, 6):
        tangent_row(i, sign, once_moved, second, factors, once[...], twice_moved, False)
    for i in span(-1, 5):
        tangent_row(i, sign, twice_moved, third, factors, twice[...], back, True)
    for i in OWN:
        adjoint_solved(i, sign, back, third, factors, once[...], out)


def backward_kernel(
    side, own, inner, outer, x1, outer_rows, inner_rows, b_outer, b_inner, once,
    packed, field,
    b0, sems,
):
    sign = side[0]
    first = state_rows(own, outer, inner)
    factors = Factors(own, outer, inner)
    lev = first.lev
    second = Rows(lev, (x1, span(-3, 7)))
    back = Rows(
        lev, (outer_rows, (0, 1)), (inner_rows, (3, 2)), (b_outer, (-1, -2)), (b_inner, (4, 5))
    )
    last = Rows(lev, (b0, span(-1, 5)))
    for i in span(-1, 5):
        adjoint_solved(i, sign, back, second, factors, once[...], last)
    outs = []
    for i in OWN:
        row = jnp.where(sign < 0.0, 3 - i, i)
        for f, value in enumerate(adjoint_row(i, sign, last, first, factors)):
            k = 4 * f + i
            packed[k * lev : (k + 1) * lev, :] = value
            copy = pltpu.make_async_copy(
                packed.at[pl.ds(k * lev, lev), :], field.at[:, f, row, :], sems.at[k]
            )
            copy.start()
            outs.append(copy)
    wait_all(outs)


def per_device(initial_state, perturbation, land_sea, relax_level, vertical_mix):
    lev, fields, rows, width = initial_state.shape
    tiles = lax.axis_size("tile")
    members = lax.axis_size("group")
    high = fields * rows * lev
    dma = pltpu.SemaphoreType.DMA
    side = (1 - 2 * (lax.axis_index("tile") & 1)).astype(jnp.float32)[None]
    across = [(i, i + 1) for i in range(1, tiles - 1, 2)]
    within = [(i, i + 1) for i in range(0, tiles, 2)]

    def swap(value, pairs):
        return lax.ppermute(value, "tile", pairs + [(j, i) for i, j in pairs])

    def buffer(n):
        return pltpu.VMEM((fields * n * lev, width), jnp.float32)

    state = run(
        pack_state_kernel,
        f32(high + 2 * rows, width),
        [SMEM, ANY, ANY, ANY],
        ANY,
        [
            dma((fields * rows,)),
            pltpu.VMEM((2, rows, width), jnp.int32),
            dma((2,)),
            pltpu.VMEM((high + 2 * rows, width), jnp.float32),
            dma((fields * rows + 1,)),
        ],
        2**20,
        60 * 2**20,
    )(side, initial_state, land_sea, relax_level)
    state_inner = swap(state, within)
    state_outer = swap(state, across)
    start = run(
        pack_field_kernel, f32(high, width), [SMEM, ANY], VMEM, [dma((fields * rows,))], nbytes=2**20
    )(side, perturbation[0])
    start_inner = swap(start, within)
    start_outer = swap(start, across)

    weights = jax.ShapeDtypeStruct((lev, 3 * lev), jnp.bfloat16)
    once, twice = run(
        inverse_kernel,
        (weights, weights),
        [SMEM],
        (VMEM, VMEM),
        [pltpu.VMEM((lev, 3 * lev), jnp.float32)],
        nbytes=2**20,
    )(vertical_mix)

    x1, x2 = run(
        trajectory_kernel,
        (f32(fields * 10 * lev, width), f32(fields * 8 * lev, width)),
        [SMEM] + [VMEM] * 4,
        (VMEM, VMEM),
        [],
        nbytes=6 * 2**20,
    )(side, state, state_inner, state_outer, once)

    outer_rows, inner_rows = run(
        forward_kernel,
        (f32(fields * 2 * lev, width), f32(fields * 2 * lev, width)),
        [SMEM] + [VMEM] * 10,
        (VMEM, VMEM),
        [buffer(10), buffer(8), buffer(6)],
        nbytes=10 * 2**20,
    )(side, state, state_inner, state_outer, start, start_inner, start_outer, x1, x2, once, twice)

    b_outer, b_inner = swap(outer_rows, across), swap(inner_rows, within)
    packed, field = run(
        backward_kernel,
        (f32(high, width), f32(lev, fields, rows, width)),
        [SMEM] + [VMEM] * 9,
        (VMEM, ANY),
        [buffer(6), dma((fields * rows,))],
        nbytes=6 * 2**20,
    )(side, state, state_inner, state_outer, x1, outer_rows, inner_rows, b_outer, b_inner, once)

    share = lax.all_to_all(
        packed.reshape(members, high // members, width), "group", 0, 0, tiled=True
    )
    products = lax.dot_general(
        share,
        share,
        (((1, 2), (1, 2)), ((), ())),
        precision=lax.Precision.HIGHEST,
        preferred_element_type=jnp.float32,
    )
    row = jnp.sum(lax.all_to_all(products, "group", 0, 0, tiled=True), axis=0)
    spread = jnp.broadcast_to(row[None], (tiles, members))
    row = jnp.sum(lax.all_to_all(spread, "tile", 0, 0, tiled=True), axis=0)
    gram = row[None] / (high * width * tiles)
    return (field[None], gram)


def solution(mesh):
    placed = (
        P(None, None, "tile", None),
        P("group", None, None, "tile", None),
        P("tile", None),
        P("tile", None),
        P(),
    )
    return jax.shard_map(
        per_device,
        mesh=mesh,
        in_specs=placed,
        out_specs=(P("group", None, None, "tile", None), P("group", None)),
        check_vma=False,
    )
```

```python
import jax
import jax.numpy as jnp
from jax import lax
from jax.experimental import pallas as pl
from jax.experimental.pallas import tpu as pltpu
from jax.sharding import PartitionSpec as P

advection = 0.2
diffusion = 0.1
drag_rate = 0.3
relaxation = 0.125

VMEM_LIMIT = 24 * 2**20

ANY = pl.BlockSpec(memory_space=pl.ANY)
VMEM = pl.BlockSpec(memory_space=pltpu.VMEM)
SMEM = pl.BlockSpec(memory_space=pltpu.SMEM)


def run(kernel, out_shape, in_specs, out_specs, scratch, nbytes, limit=VMEM_LIMIT):
    return pl.pallas_call(
        kernel,
        out_shape=out_shape,
        in_specs=in_specs,
        out_specs=out_specs,
        scratch_shapes=scratch,
        compiler_params=pltpu.CompilerParams(vmem_limit_bytes=limit),
        cost_estimate=pl.CostEstimate(flops=0, bytes_accessed=nbytes, transcendentals=0),
    )


def f32(*shape):
    return jax.ShapeDtypeStruct(shape, jnp.float32)


def start_all(copies):
    for copy in copies:
        copy.start()


def wait_all(copies):
    for copy in copies:
        copy.wait()


def place_of(f, r, rows, flipped):
    return f * rows + jnp.where(flipped, rows - 1 - r, r)


def pack_rows(src, dst, sems, flipped, base):
    lev, fields, rows, _ = src.shape
    return [
        pltpu.make_async_copy(
            src.at[:, f, r, :],
            dst.at[pl.ds(pl.multiple_of(base + place_of(f, r, rows, flipped) * lev, 8), lev), :],
            sems.at[f * rows + r],
        )
        for f in range(fields)
        for r in range(rows)
    ]


def fill_lines(ints, out, flipped, end):
    rows = ints.shape[1]
    keep = 1.0 - relaxation * ints[0].astype(jnp.float32)
    drag = drag_rate * ints[1].astype(jnp.float32)
    for k, values in enumerate((keep, drag)):
        for r in range(rows):
            other = rows - 1 - r
            line = jnp.where(flipped, values[other : other + 1], values[r : r + 1])
            out[end + k * rows + r : end + k * rows + r + 1, :] = line


def pack_kernel(side, x, p, land, relax, out, sems, ints, more_sems, staged, out_sems):
    flipped = side[0] < 0.0
    lev, fields, rows, _ = x.shape
    high = fields * rows * lev
    loads = [
        pltpu.make_async_copy(src, ints.at[k], more_sems.at[k])
        for k, src in enumerate((relax, land))
    ]
    copies = pack_rows(x, staged, sems.at[0], flipped, 0)
    copies += pack_rows(p, staged, sems.at[1], flipped, high + 2 * rows)
    start_all(loads)
    start_all(copies)
    wait_all(loads)
    fill_lines(ints, staged, flipped, high)
    pieces = [
        pl.ds(pl.multiple_of(base + place_of(f, r, rows, flipped) * lev, 8), lev)
        for base in (0, high + 2 * rows)
        for f in range(fields)
        for r in range(rows)
    ]
    pieces.append(pl.ds(high, 2 * rows))
    outs = [
        pltpu.make_async_copy(staged.at[piece], out.at[piece], out_sems.at[k])
        for k, piece in enumerate(pieces)
    ]
    outs[-1].start()
    for copy, onward in zip(copies, outs):
        copy.wait()
        onward.start()
    wait_all(outs)


def split_kernel(both, state, start, sems):
    size = state.shape[0]
    copies = [
        pltpu.make_async_copy(both.at[pl.ds(0, size)], state, sems.at[0]),
        pltpu.make_async_copy(both.at[pl.ds(size, start.shape[0])], start, sems.at[1]),
    ]
    start_all(copies)
    wait_all(copies)


def inverse_kernel(mix, once, twice, solved):
    lev = mix.shape[0]
    wide = solved.shape[1]
    lane = lax.broadcasted_iota(jnp.int32, (1, wide), 1)
    unit = lane % lev
    ratio = []
    before = None
    inv = None
    for l in range(lev):
        rhs = jnp.where(unit == l, 1.0, 0.0).astype(jnp.float32)
        if l == 0:
            diag = jnp.full((1, wide), 1.0 + mix[0], jnp.float32)
        else:
            m = mix[l - 1]
            diag = (1.0 + mix[l] + m) - (m * m) * inv
            rhs = rhs + m * before
        inv = 1.0 / diag
        before = rhs * inv
        solved[l : l + 1, :] = before
        ratio.append(inv)
    for l in reversed(range(lev - 1)):
        before = solved[l : l + 1, :] + mix[l] * ratio[l] * before
        solved[l : l + 1, :] = before
    single = solved[...]
    double = jnp.dot(
        single[:, :lev],
        single,
        precision=lax.Precision.HIGHEST,
        preferred_element_type=jnp.float32,
    )
    third = lax.broadcasted_iota(jnp.int32, (lev, wide), 1) >= 2 * lev
    for matrix, out in ((single, once), (double, twice)):
        head = matrix.astype(jnp.bfloat16)
        tail = matrix - head.astype(jnp.float32)
        out[...] = jnp.where(third, tail, head.astype(jnp.float32)).astype(jnp.bfloat16)


class Rows:
    def __init__(self, lev, *pieces):
        self.lev = lev
        self.where = {}
        for buf, rows in pieces:
            for k, i in enumerate(rows):
                for f in range(2):
                    self.where[f, i] = (buf, (f * len(rows) + k) * lev)

    def read(self, f, i):
        buf, at = self.where[f, i]
        return buf[at : at + self.lev, :]

    def write(self, f, i, value):
        buf, at = self.where[f, i]
        buf[at : at + self.lev, :] = value


OWN = (0, 1, 2, 3)
OUTER = (-1, -2, -3, -4)
INNER = (7, 6, 5, 4)


def known(own, outer, inner):
    pieces = ((own, OWN), (outer, OUTER), (inner, INNER))
    return [piece for piece in pieces if piece[0] is not None]


def state_rows(own, outer, inner):
    lev = (own.shape[0] - 8) // 8
    return Rows(lev, *known(own, outer, inner))


class Factors:
    def __init__(self, own, outer, inner):
        self.end = own.shape[0] - 8
        self.lev = self.end // 8
        self.where = {}
        for buf, rows in known(own, outer, inner):
            for k, i in enumerate(rows):
                self.where[i] = (buf, k)

    def line(self, i, kind):
        buf, k = self.where[i]
        at = self.end + 4 * kind + k
        return jnp.broadcast_to(buf[at : at + 1, :], (8, buf.shape[1]))

    def keep(self, i):
        return self.line(i, 0)

    def drag(self, i):
        return self.line(i, 1)


def tiled(block, lev):
    return jnp.concatenate([block] * (lev // 8), axis=0)


def solve(matrix, first, second):
    both = jnp.concatenate([first, second], axis=1)
    head = both.astype(jnp.bfloat16)
    tail = (both - head.astype(jnp.float32)).astype(jnp.bfloat16)
    out = jnp.dot(
        matrix, jnp.concatenate([head, tail, head], axis=0), preferred_element_type=jnp.float32
    )
    half = first.shape[1]
    return out[:, :half], out[:, half:]


def beside(value):
    lev, width = value.shape
    step = 128
    lane = lax.broadcasted_iota(jnp.int32, (lev, step), 1)
    parts = [value[:, c : c + step] for c in range(0, width, step)]
    up = [pltpu.roll(part, 1, 1) for part in parts]
    down = [pltpu.roll(part, step - 1, 1) for part in parts]
    zero = jnp.zeros_like(up[0])
    sums = []
    for k in range(len(parts)):
        west = jnp.where(lane == 0, up[k - 1] if k > 0 else zero, up[k])
        east = jnp.where(lane == step - 1, down[k + 1] if k + 1 < len(parts) else zero, down[k])
        sums.append(west + east)
    return jnp.concatenate(sums, axis=1)


def state_row(i, side, x, factors, matrix, out):
    lev = x.lev
    keep, drag = factors.keep(i), factors.drag(i)
    near = tiled(diffusion * keep, lev)
    wind = side * x.read(0, i)
    parts = []
    for f in range(2):
        centre = x.read(f, i)
        up, down = x.read(f, i + 1), x.read(f, i - 1)
        own = tiled(keep * (0.6 - drag) if f == 0 else 0.6 * keep, lev)
        around = (up + down) + beside(centre) - wind * (up - down)
        parts.append(own * centre + near * around)
    for f, value in enumerate(solve(matrix, *parts)):
        out.write(f, i, value)


def tangent_row(i, side, d, x, factors, matrix, out, damp):
    lev = x.lev
    keep, drag = factors.keep(i), factors.drag(i)
    near = tiled(diffusion * keep, lev)
    wind = side * x.read(0, i)
    du = side * d.read(0, i)
    parts = []
    for f in range(2):
        centre = d.read(f, i)
        up, down = d.read(f, i + 1), d.read(f, i - 1)
        slope = x.read(f, i + 1) - x.read(f, i - 1)
        own = tiled(keep * (0.6 - drag) if f == 0 else 0.6 * keep, lev)
        around = (up + down) + beside(centre) - wind * (up - down) - du * slope
        parts.append(own * centre + near * around)
    for f, value in enumerate(solve(matrix, *parts)):
        out.write(f, i, value * tiled(keep, lev) if damp else value)


def adjoint_row(i, side, b, x, factors):
    lev = x.lev
    drag = factors.drag(i)
    more = 1.0 + side * x.read(0, i + 1)
    less = 1.0 - side * x.read(0, i - 1)
    parts = []
    sloped = 0.0
    for f in range(2):
        centre = b.read(f, i)
        sloped = sloped + centre * (x.read(f, i + 1) - x.read(f, i - 1))
        around = more * b.read(f, i + 1) + less * b.read(f, i - 1) + beside(centre)
        parts.append((centre, around))
    wind_part = tiled(0.6 - drag, lev) * parts[0][0] + diffusion * (parts[0][1] - side * sloped)
    heat_part = 0.6 * parts[1][0] + diffusion * parts[1][1]
    return wind_part, heat_part


def adjoint_solved(i, side, b, x, factors, matrix, out):
    keep = tiled(factors.keep(i), x.lev)
    for f, value in enumerate(solve(matrix, *adjoint_row(i, side, b, x, factors))):
        out.write(f, i, value * keep)


def span(first, last):
    return tuple(range(first, last))


def forward(side, state, start, factors, xs, moved, once, twice, ranges):
    for i in ranges[0]:
        state_row(i, side, state, factors, once, xs[0])
    for i in ranges[1]:
        state_row(i, side, xs[0], factors, once, xs[1])
    for i in ranges[2]:
        tangent_row(i, side, start, state, factors, once, moved[0], False)
    for i in ranges[3]:
        tangent_row(i, side, moved[0], xs[0], factors, once, moved[1], False)
    for i in ranges[4]:
        tangent_row(i, side, moved[1], xs[1], factors, twice, moved[2], True)


def inner_forward_kernel(
    side, own, inner, p_own, p_inner, once, twice,
    x1, x2, t1, t2, b2,
):
    state = state_rows(own, None, inner)
    lev = state.lev
    forward(
        side[0],
        state,
        Rows(lev, (p_own, OWN), (p_inner, INNER)),
        Factors(own, None, inner),
        (Rows(lev, (x1, span(1, 7))), Rows(lev, (x2, span(2, 6)))),
        (Rows(lev, (t1, span(1, 7))), Rows(lev, (t2, span(2, 6))), Rows(lev, (b2, span(3, 5)))),
        once[...],
        twice[...],
        (span(1, 7), span(2, 6), span(1, 7), span(2, 6), span(3, 5)),
    )


def forward_kernel(
    side, own, p_own, both_outer, x1_in, x2_in, t1_in, t2_in, b2_in, once, twice,
    outer_rows, inner_rows, x1,
    x2, t1, t2, b2,
):
    sign = side[0]
    size = own.shape[0]
    outer = both_outer.at[pl.ds(0, size)]
    p_outer = both_outer.at[pl.ds(size, p_own.shape[0])]
    state = state_rows(own, outer, None)
    factors = Factors(own, outer, None)
    lev = state.lev
    xs = (
        Rows(lev, (x1, span(-3, 1)), (x1_in, span(1, 7))),
        Rows(lev, (x2, span(-2, 2)), (x2_in, span(2, 6))),
    )
    moved = (
        Rows(lev, (t1, span(-3, 1)), (t1_in, span(1, 7))),
        Rows(lev, (t2, span(-2, 2)), (t2_in, span(2, 6))),
        Rows(lev, (b2, span(-1, 3)), (b2_in, span(3, 5))),
    )
    forward(
        sign,
        state,
        Rows(lev, (p_own, OWN), (p_outer, OUTER)),
        factors,
        xs,
        moved,
        once[...],
        twice[...],
        (span(-3, 1), span(-2, 2), span(-3, 1), span(-2, 2), span(-1, 3)),
    )
    out = Rows(lev, (outer_rows, (0, 1)), (inner_rows, (3, 2)))
    for i in OWN:
        adjoint_solved(i, sign, moved[2], xs[1], factors, once[...], out)


def backward_kernel(
    side, own, inner, both_outer, x1, x1_in, outer_rows, inner_rows, b_outer, b_inner, once,
    packed, field,
    b0, sems,
):
    sign = side[0]
    outer = both_outer.at[pl.ds(0, own.shape[0])]
    state = state_rows(own, outer, inner)
    factors = Factors(own, outer, inner)
    lev = state.lev
    second = Rows(lev, (x1, span(-3, 1)), (x1_in, span(1, 7)))
    back = Rows(
        lev, (outer_rows, (0, 1)), (inner_rows, (3, 2)), (b_outer, (-1, -2)), (b_inner, (4, 5))
    )
    last = Rows(lev, (b0, span(-1, 5)))
    for i in span(-1, 5):
        adjoint_solved(i, sign, back, second, factors, once[...], last)
    copies = []
    for i in OWN:
        row = jnp.where(sign < 0.0, 3 - i, i)
        for f, value in enumerate(adjoint_row(i, sign, last, state, factors)):
            k = 4 * f + i
            packed[k * lev : (k + 1) * lev, :] = value
            copies.append(
                pltpu.make_async_copy(
                    packed.at[pl.ds(k * lev, lev), :], field.at[:, f, row, :], sems.at[k]
                )
            )
            copies[-1].start()
    wait_all(copies)


def per_device(initial_state, perturbation, land_sea, relax_level, vertical_mix):
    lev, fields, rows, width = initial_state.shape
    tiles = lax.axis_size("tile")
    members = lax.axis_size("group")
    high = fields * rows * lev
    dma = pltpu.SemaphoreType.DMA
    side = (1 - 2 * (lax.axis_index("tile") & 1)).astype(jnp.float32)[None]
    across = [(i, i + 1) for i in range(1, tiles - 1, 2)]
    within = [(i, i + 1) for i in range(0, tiles, 2)]

    def swap(value, pairs):
        return lax.ppermute(value, "tile", pairs + [(j, i) for i, j in pairs])

    def buffer(n):
        return pltpu.VMEM((fields * n * lev, width), jnp.float32)

    def rows_of(n):
        return f32(fields * n * lev, width)

    both = run(
        pack_kernel,
        f32(2 * high + 2 * rows, width),
        [SMEM] + [ANY] * 4,
        ANY,
        [
            dma((2, fields * rows)),
            pltpu.VMEM((2, rows, width), jnp.int32),
            dma((2,)),
            pltpu.VMEM((2 * high + 2 * rows, width), jnp.float32),
            dma((2 * fields * rows + 1,)),
        ],
        2**20,
        60 * 2**20,
    )(side, initial_state, perturbation[0], land_sea, relax_level)
    both_outer = swap(both, across)
    state, start = run(
        split_kernel,
        (f32(high + 2 * rows, width), f32(high, width)),
        [ANY],
        (VMEM, VMEM),
        [dma((2,))],
        nbytes=2**18,
    )(both)
    state_inner = swap(state, within)
    start_inner = swap(start, within)

    weights = jax.ShapeDtypeStruct((lev, 3 * lev), jnp.bfloat16)
    once, twice = run(
        inverse_kernel,
        (weights, weights),
        [SMEM],
        (VMEM, VMEM),
        [pltpu.VMEM((lev, 3 * lev), jnp.float32)],
        nbytes=2**18,
    )(vertical_mix)

    x1_in, x2_in, t1, t2, b2 = run(
        inner_forward_kernel,
        (rows_of(6), rows_of(4), rows_of(6), rows_of(4), rows_of(2)),
        [SMEM] + [VMEM] * 6,
        (VMEM,) * 5,
        [],
        nbytes=2**18,
    )(side, state, state_inner, start, start_inner, once, twice)
    outer_rows, inner_rows, x1 = run(
        forward_kernel,
        (rows_of(2), rows_of(2), rows_of(4)),
        [SMEM] + [VMEM] * 10,
        (VMEM,) * 3,
        [buffer(4)] * 4,
        nbytes=2**20,
    )(side, state, start, both_outer, x1_in, x2_in, t1, t2, b2, once, twice)

    b_outer, b_inner = swap(outer_rows, across), swap(inner_rows, within)
    packed, field = run(
        backward_kernel,
        (f32(high, width), f32(lev, fields, rows, width)),
        [SMEM] + [VMEM] * 10,
        (VMEM, ANY),
        [buffer(6), dma((fields * rows,))],
        nbytes=2**20,
    )(side, state, state_inner, both_outer, x1, x1_in, outer_rows, inner_rows, b_outer, b_inner, once)

    share = lax.all_to_all(
        packed.reshape(members, high // members, width), "group", 0, 0, tiled=True
    )
    products = lax.dot_general(
        share,
        share,
        (((1, 2), (1, 2)), ((), ())),
        precision=lax.Precision.HIGHEST,
        preferred_element_type=jnp.float32,
    )
    row = jnp.sum(lax.all_to_all(products, "group", 0, 0, tiled=True), axis=0)
    spread = jnp.broadcast_to(row[None], (tiles, members))
    row = jnp.sum(lax.all_to_all(spread, "tile", 0, 0, tiled=True), axis=0)
    gram = row[None] / (high * width * tiles)
    return (field[None], gram)


def solution(mesh):
    placed = (
        P(None, None, "tile", None),
        P("group", None, None, "tile", None),
        P("tile", None),
        P("tile", None),
        P(),
    )
    return jax.shard_map(
        per_device,
        mesh=mesh,
        in_specs=placed,
        out_specs=(P("group", None, None, "tile", None), P("group", None)),
        check_vma=False,
    )
```

```python
import jax
import jax.numpy as jnp
from jax import lax
from jax.experimental import pallas as pl
from jax.experimental.pallas import tpu as pltpu
from jax.sharding import PartitionSpec as P

advection = 0.2
diffusion = 0.1
drag_rate = 0.3
relaxation = 0.125

VMEM_LIMIT = 24 * 2**20

ANY = pl.BlockSpec(memory_space=pl.ANY)
VMEM = pl.BlockSpec(memory_space=pltpu.VMEM)
SMEM = pl.BlockSpec(memory_space=pltpu.SMEM)


def run(kernel, out_shape, in_specs, out_specs, scratch, nbytes, limit=VMEM_LIMIT):
    return pl.pallas_call(
        kernel,
        out_shape=out_shape,
        in_specs=in_specs,
        out_specs=out_specs,
        scratch_shapes=scratch,
        compiler_params=pltpu.CompilerParams(vmem_limit_bytes=limit),
        cost_estimate=pl.CostEstimate(flops=0, bytes_accessed=nbytes, transcendentals=0),
    )


def f32(*shape):
    return jax.ShapeDtypeStruct(shape, jnp.float32)


def start_all(copies):
    for copy in copies:
        copy.start()


def wait_all(copies):
    for copy in copies:
        copy.wait()


def place_of(f, r, rows, flipped):
    return f * rows + jnp.where(flipped, rows - 1 - r, r)


def pack_rows(src, dst, sems, flipped, base):
    lev, fields, rows, _ = src.shape
    return [
        pltpu.make_async_copy(
            src.at[:, f, r, :],
            dst.at[pl.ds(pl.multiple_of(base + place_of(f, r, rows, flipped) * lev, 8), lev), :],
            sems.at[f * rows + r],
        )
        for f in range(fields)
        for r in range(rows)
    ]


def fill_lines(ints, out, flipped, end):
    rows = ints.shape[1]
    keep = 1.0 - relaxation * ints[0].astype(jnp.float32)
    drag = drag_rate * ints[1].astype(jnp.float32)
    for k, values in enumerate((keep, drag)):
        for r in range(rows):
            other = rows - 1 - r
            line = jnp.where(flipped, values[other : other + 1], values[r : r + 1])
            out[end + k * rows + r : end + k * rows + r + 1, :] = line


def pack_kernel(side, x, p, land, relax, out, deep, sems, ints, more_sems, staged, out_sems):
    flipped = side[0] < 0.0
    lev, fields, rows, _ = x.shape
    high = fields * rows * lev
    loads = [
        pltpu.make_async_copy(src, ints.at[k], more_sems.at[k])
        for k, src in enumerate((relax, land))
    ]
    copies = pack_rows(x, staged, sems.at[0], flipped, 0)
    copies += pack_rows(p, staged, sems.at[1], flipped, high + 2 * rows)
    start_all(loads)
    start_all(copies)
    wait_all(loads)
    fill_lines(ints, staged, flipped, high)
    pieces = [
        pl.ds(pl.multiple_of(base + place_of(f, r, rows, flipped) * lev, 8), lev)
        for base in (0, high + 2 * rows)
        for f in range(fields)
        for r in range(rows)
    ]
    pieces.append(pl.ds(high, 2 * rows))
    outs = [
        pltpu.make_async_copy(staged.at[piece], out.at[piece], out_sems.at[k])
        for k, piece in enumerate(pieces)
    ]
    outs[-1].start()
    for copy, onward in zip(copies, outs):
        copy.wait()
        onward.start()
    two, four = 2 * lev, 4 * lev
    shift = 2 * rows + fields * two
    inner = [(f * four + two, f * two, two) for f in range(fields)]
    inner += [(high, fields * two, 2 * rows)]
    inner += [(high + 2 * rows + f * four + two, shift + f * two, two) for f in range(fields)]
    for k, (at, to, size) in enumerate(inner):
        outs.append(
            pltpu.make_async_copy(
                staged.at[pl.ds(at, size)], deep.at[pl.ds(to, size)], out_sems.at[len(pieces) + k]
            )
        )
        outs[-1].start()
    wait_all(outs)


def relay_kernel(both, after, state_part, start_part, sems):
    two = start_part.shape[0] // 2
    ends = state_part.shape[0] - 2 * two
    high = (both.shape[0] - ends) // 2
    moves = [(0, state_part, 0, two), (2 * two, state_part, two, two)]
    moves += [(high, state_part, 2 * two, ends)]
    moves += [(high + ends, start_part, 0, two), (high + ends + 2 * two, start_part, two, two)]
    copies = [
        pltpu.make_async_copy(both.at[pl.ds(at, size)], dst.at[pl.ds(to, size)], sems.at[k])
        for k, (at, dst, to, size) in enumerate(moves)
    ]
    start_all(copies)
    wait_all(copies)


def split_kernel(both, state, start, sems):
    size = state.shape[0]
    copies = [
        pltpu.make_async_copy(both.at[pl.ds(0, size)], state, sems.at[0]),
        pltpu.make_async_copy(both.at[pl.ds(size, start.shape[0])], start, sems.at[1]),
    ]
    start_all(copies)
    wait_all(copies)


def inverse_kernel(mix, once, twice, solved):
    lev = mix.shape[0]
    wide = solved.shape[1]
    lane = lax.broadcasted_iota(jnp.int32, (1, wide), 1)
    unit = lane % lev
    ratio = []
    before = None
    inv = None
    for l in range(lev):
        rhs = jnp.where(unit == l, 1.0, 0.0).astype(jnp.float32)
        if l == 0:
            diag = jnp.full((1, wide), 1.0 + mix[0], jnp.float32)
        else:
            m = mix[l - 1]
            diag = (1.0 + mix[l] + m) - (m * m) * inv
            rhs = rhs + m * before
        inv = 1.0 / diag
        before = rhs * inv
        solved[l : l + 1, :] = before
        ratio.append(inv)
    for l in reversed(range(lev - 1)):
        before = solved[l : l + 1, :] + mix[l] * ratio[l] * before
        solved[l : l + 1, :] = before
    single = solved[...]
    double = jnp.dot(
        single[:, :lev],
        single,
        precision=lax.Precision.HIGHEST,
        preferred_element_type=jnp.float32,
    )
    third = lax.broadcasted_iota(jnp.int32, (lev, wide), 1) >= 2 * lev
    for matrix, out in ((single, once), (double, twice)):
        head = matrix.astype(jnp.bfloat16)
        tail = matrix - head.astype(jnp.float32)
        out[...] = jnp.where(third, tail, head.astype(jnp.float32)).astype(jnp.bfloat16)


class Rows:
    def __init__(self, lev, *pieces):
        self.lev = lev
        self.where = {}
        for buf, rows in pieces:
            for k, i in enumerate(rows):
                for f in range(2):
                    self.where[f, i] = (buf, (f * len(rows) + k) * lev)

    def read(self, f, i):
        buf, at = self.where[f, i]
        return buf[at : at + self.lev, :]

    def write(self, f, i, value):
        buf, at = self.where[f, i]
        buf[at : at + self.lev, :] = value


OWN = (0, 1, 2, 3)
OUTER = (-1, -2, -3, -4)
INNER = (7, 6, 5, 4)
DEEP = (-6, -5)
FAR = (8, 9)


def span(first, last):
    return tuple(range(first, last))


class Factors:
    def __init__(self, *pieces):
        self.where = {}
        for buf, rows, first in pieces:
            for k, i in enumerate(rows):
                self.where[i] = (buf, first + k)

    def line(self, i, kind):
        buf, k = self.where[i]
        at = buf.shape[0] - 8 + 4 * kind + k
        return jnp.broadcast_to(buf[at : at + 1, :], (8, buf.shape[1]))

    def keep(self, i):
        return self.line(i, 0)

    def drag(self, i):
        return self.line(i, 1)


def tiled(block, lev):
    return jnp.concatenate([block] * (lev // 8), axis=0)


def solve(matrix, first, second):
    both = jnp.concatenate([first, second], axis=1)
    head = both.astype(jnp.bfloat16)
    tail = (both - head.astype(jnp.float32)).astype(jnp.bfloat16)
    out = jnp.dot(
        matrix, jnp.concatenate([head, tail, head], axis=0), preferred_element_type=jnp.float32
    )
    half = first.shape[1]
    return out[:, :half], out[:, half:]


def beside(value):
    lev, width = value.shape
    step = 128
    lane = lax.broadcasted_iota(jnp.int32, (lev, step), 1)
    parts = [value[:, c : c + step] for c in range(0, width, step)]
    up = [pltpu.roll(part, 1, 1) for part in parts]
    down = [pltpu.roll(part, step - 1, 1) for part in parts]
    zero = jnp.zeros_like(up[0])
    sums = []
    for k in range(len(parts)):
        west = jnp.where(lane == 0, up[k - 1] if k > 0 else zero, up[k])
        east = jnp.where(lane == step - 1, down[k + 1] if k + 1 < len(parts) else zero, down[k])
        sums.append(west + east)
    return jnp.concatenate(sums, axis=1)


def state_row(i, side, x, factors, matrix, out):
    lev = x.lev
    keep, drag = factors.keep(i), factors.drag(i)
    near = tiled(diffusion * keep, lev)
    wind = side * x.read(0, i)
    parts = []
    for f in range(2):
        centre = x.read(f, i)
        up, down = x.read(f, i + 1), x.read(f, i - 1)
        own = tiled(keep * (0.6 - drag) if f == 0 else 0.6 * keep, lev)
        around = (up + down) + beside(centre) - wind * (up - down)
        parts.append(own * centre + near * around)
    for f, value in enumerate(solve(matrix, *parts)):
        out.write(f, i, value)


def tangent_row(i, side, d, x, factors, matrix, out, damp):
    lev = x.lev
    keep, drag = factors.keep(i), factors.drag(i)
    near = tiled(diffusion * keep, lev)
    wind = side * x.read(0, i)
    du = side * d.read(0, i)
    parts = []
    for f in range(2):
        centre = d.read(f, i)
        up, down = d.read(f, i + 1), d.read(f, i - 1)
        slope = x.read(f, i + 1) - x.read(f, i - 1)
        own = tiled(keep * (0.6 - drag) if f == 0 else 0.6 * keep, lev)
        around = (up + down) + beside(centre) - wind * (up - down) - du * slope
        parts.append(own * centre + near * around)
    for f, value in enumerate(solve(matrix, *parts)):
        out.write(f, i, value * tiled(keep, lev) if damp else value)


def adjoint_row(i, side, b, x, factors):
    lev = x.lev
    drag = factors.drag(i)
    more = 1.0 + side * x.read(0, i + 1)
    less = 1.0 - side * x.read(0, i - 1)
    parts = []
    sloped = 0.0
    for f in range(2):
        centre = b.read(f, i)
        sloped = sloped + centre * (x.read(f, i + 1) - x.read(f, i - 1))
        around = more * b.read(f, i + 1) + less * b.read(f, i - 1) + beside(centre)
        parts.append((centre, around))
    wind_part = tiled(0.6 - drag, lev) * parts[0][0] + diffusion * (parts[0][1] - side * sloped)
    heat_part = 0.6 * parts[1][0] + diffusion * parts[1][1]
    return wind_part, heat_part


def adjoint_solved(i, side, b, x, factors, matrix, out):
    keep = tiled(factors.keep(i), x.lev)
    for f, value in enumerate(solve(matrix, *adjoint_row(i, side, b, x, factors))):
        out.write(f, i, value * keep)


class Fields:
    def __init__(self, lev, **pieces):
        self.rows = {name: Rows(lev, *piece) for name, piece in pieces.items()}

    def __getattr__(self, name):
        return self.rows[name]


def forward(side, rows, factors, once, twice, ranges):
    for i in ranges[0]:
        state_row(i, side, rows.x0, factors, once, rows.x1)
    for i in ranges[1]:
        state_row(i, side, rows.x1, factors, once, rows.x2)
    for i in ranges[2]:
        tangent_row(i, side, rows.p, rows.x0, factors, once, rows.t1, False)
    for i in ranges[3]:
        tangent_row(i, side, rows.t1, rows.x1, factors, once, rows.t2, False)
    for i in ranges[4]:
        tangent_row(i, side, rows.t2, rows.x2, factors, twice, rows.b2, True)
    for i in ranges[5]:
        adjoint_solved(i, side, rows.b2, rows.x2, factors, once, rows.b1)


def own_kernel(
    side, own, inner, p_own, p_inner, once, twice,
    x1, x2, t1, t2, b2,
):
    lev = p_own.shape[0] // 8
    rows = Fields(
        lev,
        x0=((own, OWN), (inner, INNER)),
        p=((p_own, OWN), (p_inner, INNER)),
        x1=((x1, span(1, 7)),),
        x2=((x2, span(2, 6)),),
        t1=((t1, span(1, 7)),),
        t2=((t2, span(2, 6)),),
        b2=((b2, span(3, 5)),),
    )
    forward(
        side[0],
        rows,
        Factors((own, OWN, 0), (inner, INNER, 0)),
        once[...],
        twice[...],
        (span(1, 7), span(2, 6), span(1, 7), span(2, 6), span(3, 5), ()),
    )


def outer_kernel(
    side, own, p_own, both_outer, x1_own, x2_own, t1_own, t2_own, b2_own, once, twice,
    x1, x2, t1, t2, b2, b1,
):
    size = own.shape[0]
    outer = both_outer.at[pl.ds(0, size)]
    p_outer = both_outer.at[pl.ds(size, p_own.shape[0])]
    rows = Fields(
        p_own.shape[0] // 8,
        x0=((own, OWN), (outer, OUTER)),
        p=((p_own, OWN), (p_outer, OUTER)),
        x1=((x1, span(-3, 1)), (x1_own, span(1, 7))),
        x2=((x2, span(-2, 2)), (x2_own, span(2, 6))),
        t1=((t1, span(-3, 1)), (t1_own, span(1, 7))),
        t2=((t2, span(-2, 2)), (t2_own, span(2, 6))),
        b2=((b2, span(-1, 3)), (b2_own, span(3, 5))),
        b1=((b1, OWN),),
    )
    forward(
        side[0],
        rows,
        Factors((own, OWN, 0), (outer, OUTER, 0)),
        once[...],
        twice[...],
        (span(-3, 1), span(-2, 2), span(-3, 1), span(-2, 2), span(-1, 3), OWN),
    )


def far_kernel(
    side, inner, p_inner, far, p_far, x1_own, x2_own, t1_own, t2_own, b2_own, once, twice,
    b1,
    x1, x2, t1, t2, b2,
):
    rows = Fields(
        p_inner.shape[0] // 8,
        x0=((inner, INNER), (far, FAR)),
        p=((p_inner, INNER), (p_far, FAR)),
        x1=((x1_own, span(1, 7)), (x1, (7, 8))),
        x2=((x2_own, span(2, 6)), (x2, (6, 7))),
        t1=((t1_own, span(1, 7)), (t1, (7, 8))),
        t2=((t2_own, span(2, 6)), (t2, (6, 7))),
        b2=((b2_own, span(3, 5)), (b2, (5, 6))),
        b1=((b1, (4, 5)),),
    )
    forward(
        side[0],
        rows,
        Factors((inner, INNER, 0), (far, FAR, 0)),
        once[...],
        twice[...],
        ((7, 8), (6, 7), (7, 8), (6, 7), (5, 6), (4, 5)),
    )


def last_kernel(
    side, own, inner, both_outer, deep, x1_own, x1_outer, x2_outer, t1_outer, t2_outer,
    b2_outer, b1_own, b1_far, once, twice,
    packed, field,
    x1, x2, t1, t2, b2, b1, b0, sems,
):
    sign = side[0]
    high = packed.shape[0]
    lev = high // 8
    size = own.shape[0]
    outer = both_outer.at[pl.ds(0, size)]
    p_outer = both_outer.at[pl.ds(size, high)]
    part = high // 2 + size - high
    deeper = deep.at[pl.ds(0, part)]
    p_deeper = deep.at[pl.ds(part, high // 2)]
    rows = Fields(
        lev,
        x0=((own, OWN), (inner, INNER), (outer, OUTER), (deeper, DEEP)),
        p=((p_outer, OUTER), (p_deeper, DEEP)),
        x1=((x1, (-5, -4)), (x1_outer, span(-3, 1)), (x1_own, span(1, 7))),
        x2=((x2, (-4, -3)), (x2_outer, span(-2, 2))),
        t1=((t1, (-5, -4)), (t1_outer, span(-3, 1))),
        t2=((t2, (-4, -3)), (t2_outer, span(-2, 2))),
        b2=((b2, (-3, -2)), (b2_outer, span(-1, 3))),
        b1=((b1, (-2, -1)), (b1_own, OWN), (b1_far, (4, 5))),
        b0=((b0, span(-1, 5)),),
    )
    factors = Factors((own, OWN, 0), (inner, INNER, 0), (outer, OUTER, 0), (deeper, DEEP, 2))
    forward(
        sign,
        rows,
        factors,
        once[...],
        twice[...],
        ((-5, -4), (-4, -3), (-5, -4), (-4, -3), (-3, -2), (-2, -1)),
    )
    for i in span(-1, 5):
        adjoint_solved(i, sign, rows.b1, rows.x1, factors, once[...], rows.b0)
    copies = []
    for i in OWN:
        row = jnp.where(sign < 0.0, 3 - i, i)
        for f, value in enumerate(adjoint_row(i, sign, rows.b0, rows.x0, factors)):
            k = 4 * f + i
            packed[k * lev : (k + 1) * lev, :] = value
            copies.append(
                pltpu.make_async_copy(
                    packed.at[pl.ds(k * lev, lev), :], field.at[:, f, row, :], sems.at[k]
                )
            )
            copies[-1].start()
    wait_all(copies)


def per_device(initial_state, perturbation, land_sea, relax_level, vertical_mix):
    lev, fields, rows, width = initial_state.shape
    tiles = lax.axis_size("tile")
    members = lax.axis_size("group")
    high = fields * rows * lev
    dma = pltpu.SemaphoreType.DMA
    side = (1 - 2 * (lax.axis_index("tile") & 1)).astype(jnp.float32)[None]
    across = [(i, i + 1) for i in range(1, tiles - 1, 2)]
    beyond = [(i, i + 2) for i in range(0, tiles - 2, 2)]
    beyond += [(i + 2, i) for i in range(1, tiles - 2, 2)]
    within = [(i, i + 1) for i in range(0, tiles, 2)]

    def swap(value, pairs):
        return lax.ppermute(value, "tile", pairs + [(j, i) for i, j in pairs])

    def buffer(n):
        return pltpu.VMEM((fields * n * lev, width), jnp.float32)

    def rows_of(n):
        return f32(fields * n * lev, width)

    both, deep = run(
        pack_kernel,
        (f32(2 * high + 2 * rows, width), f32(high + 2 * rows, width)),
        [SMEM] + [ANY] * 4,
        (ANY, ANY),
        [
            dma((2, fields * rows)),
            pltpu.VMEM((2, rows, width), jnp.int32),
            dma((2,)),
            pltpu.VMEM((2 * high + 2 * rows, width), jnp.float32),
            dma((2 * fields * rows + 6,)),
        ],
        2**20,
        60 * 2**20,
    )(side, initial_state, perturbation[0], land_sea, relax_level)
    both_outer = swap(both, across)
    deep = lax.ppermute(deep, "tile", beyond)
    state, start = run(
        split_kernel,
        (f32(high + 2 * rows, width), f32(high, width)),
        [ANY],
        (VMEM, VMEM),
        [dma((2,))],
        nbytes=2**18,
    )(both)
    state_inner = swap(state, within)
    start_inner = swap(start, within)

    weights = jax.ShapeDtypeStruct((lev, 3 * lev), jnp.bfloat16)
    once, twice = run(
        inverse_kernel,
        (weights, weights),
        [SMEM],
        (VMEM, VMEM),
        [pltpu.VMEM((lev, 3 * lev), jnp.float32)],
        nbytes=2**18,
    )(vertical_mix)

    x1_own, x2_own, t1_own, t2_own, b2_own = run(
        own_kernel,
        (rows_of(6), rows_of(4), rows_of(6), rows_of(4), rows_of(2)),
        [SMEM] + [VMEM] * 6,
        (VMEM,) * 5,
        [],
        nbytes=0,
    )(side, state, state_inner, start, start_inner, once, twice)

    far, p_far = run(
        relay_kernel,
        (f32(high // 2 + 2 * rows, width), f32(high // 2, width)),
        [ANY, ANY],
        (VMEM, VMEM),
        [dma((5,))],
        nbytes=0,
    )(both_outer, b2_own)
    far, p_far = swap(far, within), swap(p_far, within)

    x1_outer, x2_outer, t1_outer, t2_outer, b2_outer, b1_own = run(
        outer_kernel,
        (rows_of(4),) * 6,
        [SMEM] + [VMEM] * 10,
        (VMEM,) * 6,
        [],
        nbytes=0,
    )(side, state, start, both_outer, x1_own, x2_own, t1_own, t2_own, b2_own, once, twice)
    b1_far = run(
        far_kernel,
        rows_of(2),
        [SMEM] + [VMEM] * 11,
        VMEM,
        [buffer(2)] * 5,
        nbytes=0,
    )(
        side, state_inner, start_inner, far, p_far, x1_own, x2_own, t1_own, t2_own, b2_own,
        once, twice,
    )
    packed, field = run(
        last_kernel,
        (f32(high, width), f32(lev, fields, rows, width)),
        [SMEM] + [VMEM] * 14,
        (VMEM, ANY),
        [buffer(2)] * 6 + [buffer(6), dma((fields * rows,))],
        nbytes=0,
    )(
        side, state, state_inner, both_outer, deep, x1_own, x1_outer, x2_outer, t1_outer,
        t2_outer, b2_outer, b1_own, b1_far, once, twice,
    )

    share = lax.all_to_all(
        packed.reshape(members, high // members, width), "group", 0, 0, tiled=True
    )
    products = lax.dot_general(
        share,
        share,
        (((1, 2), (1, 2)), ((), ())),
        precision=lax.Precision.HIGHEST,
        preferred_element_type=jnp.float32,
    )
    row = jnp.sum(lax.all_to_all(products, "group", 0, 0, tiled=True), axis=0)
    spread = jnp.broadcast_to(row[None], (tiles, members))
    row = jnp.sum(lax.all_to_all(spread, "tile", 0, 0, tiled=True), axis=0)
    gram = row[None] / (high * width * tiles)
    return (field[None], gram)


def solution(mesh):
    placed = (
        P(None, None, "tile", None),
        P("group", None, None, "tile", None),
        P("tile", None),
        P("tile", None),
        P(),
    )
    return jax.shard_map(
        per_device,
        mesh=mesh,
        in_specs=placed,
        out_specs=(P("group", None, None, "tile", None), P("group", None)),
        check_vma=False,
    )
```

```python
import jax
import jax.numpy as jnp
from jax import lax
from jax.experimental import pallas as pl
from jax.experimental.pallas import tpu as pltpu
from jax.sharding import PartitionSpec as P

advection = 0.2
diffusion = 0.1
drag_rate = 0.3
relaxation = 0.125

VMEM_LIMIT = 24 * 2**20

ANY = pl.BlockSpec(memory_space=pl.ANY)
VMEM = pl.BlockSpec(memory_space=pltpu.VMEM)
SMEM = pl.BlockSpec(memory_space=pltpu.SMEM)


def run(kernel, out_shape, in_specs, out_specs, scratch, nbytes, limit=VMEM_LIMIT):
    return pl.pallas_call(
        kernel,
        out_shape=out_shape,
        in_specs=in_specs,
        out_specs=out_specs,
        scratch_shapes=scratch,
        compiler_params=pltpu.CompilerParams(vmem_limit_bytes=limit),
        cost_estimate=pl.CostEstimate(flops=0, bytes_accessed=nbytes, transcendentals=0),
    )


def f32(*shape):
    return jax.ShapeDtypeStruct(shape, jnp.float32)


def start_all(copies):
    for copy in copies:
        copy.start()


def wait_all(copies):
    for copy in copies:
        copy.wait()


def place_of(f, r, rows, flipped):
    return f * rows + jnp.where(flipped, rows - 1 - r, r)


def pack_rows(src, dst, sems, flipped, base):
    lev, fields, rows, _ = src.shape
    return [
        pltpu.make_async_copy(
            src.at[:, f, r, :],
            dst.at[pl.ds(pl.multiple_of(base + place_of(f, r, rows, flipped) * lev, 8), lev), :],
            sems.at[f * rows + r],
        )
        for f in range(fields)
        for r in range(rows)
    ]


def fill_lines(ints, out, flipped, end):
    rows = ints.shape[1]
    keep = 1.0 - relaxation * ints[0].astype(jnp.float32)
    drag = drag_rate * ints[1].astype(jnp.float32)
    for k, values in enumerate((keep, drag)):
        for r in range(rows):
            other = rows - 1 - r
            line = jnp.where(flipped, values[other : other + 1], values[r : r + 1])
            out[end + k * rows + r : end + k * rows + r + 1, :] = line


def pack_kernel(side, x, p, land, relax, out, sems, ints, more_sems, staged, out_sems):
    flipped = side[0] < 0.0
    lev, fields, rows, _ = x.shape
    high = fields * rows * lev
    loads = [
        pltpu.make_async_copy(src, ints.at[k], more_sems.at[k])
        for k, src in enumerate((relax, land))
    ]
    copies = pack_rows(x, staged, sems.at[0], flipped, 0)
    copies += pack_rows(p, staged, sems.at[1], flipped, high + 2 * rows)
    start_all(loads)
    start_all(copies)
    wait_all(loads)
    fill_lines(ints, staged, flipped, high)
    pieces = [
        pl.ds(pl.multiple_of(base + place_of(f, r, rows, flipped) * lev, 8), lev)
        for base in (0, high + 2 * rows)
        for f in range(fields)
        for r in range(rows)
    ]
    pieces.append(pl.ds(high, 2 * rows))
    outs = [
        pltpu.make_async_copy(staged.at[piece], out.at[piece], out_sems.at[k])
        for k, piece in enumerate(pieces)
    ]
    outs[-1].start()
    for copy, onward in zip(copies, outs):
        copy.wait()
        onward.start()
    wait_all(outs)


def split_kernel(both, state, start, sems):
    size = state.shape[0]
    copies = [
        pltpu.make_async_copy(both.at[pl.ds(0, size)], state, sems.at[0]),
        pltpu.make_async_copy(both.at[pl.ds(size, start.shape[0])], start, sems.at[1]),
    ]
    start_all(copies)
    wait_all(copies)


def inverse_kernel(mix, once, twice, solved):
    lev = mix.shape[0]
    wide = solved.shape[1]
    lane = lax.broadcasted_iota(jnp.int32, (1, wide), 1)
    unit = lane % lev
    ratio = []
    before = None
    inv = None
    for l in range(lev):
        rhs = jnp.where(unit == l, 1.0, 0.0).astype(jnp.float32)
        if l == 0:
            diag = jnp.full((1, wide), 1.0 + mix[0], jnp.float32)
        else:
            m = mix[l - 1]
            diag = (1.0 + mix[l] + m) - (m * m) * inv
            rhs = rhs + m * before
        inv = 1.0 / diag
        before = rhs * inv
        solved[l : l + 1, :] = before
        ratio.append(inv)
    for l in reversed(range(lev - 1)):
        before = solved[l : l + 1, :] + mix[l] * ratio[l] * before
        solved[l : l + 1, :] = before
    single = solved[...]
    double = jnp.dot(
        single[:, :lev],
        single,
        precision=lax.Precision.HIGHEST,
        preferred_element_type=jnp.float32,
    )
    third = lax.broadcasted_iota(jnp.int32, (lev, wide), 1) >= 2 * lev
    for matrix, out in ((single, once), (double, twice)):
        head = matrix.astype(jnp.bfloat16)
        tail = matrix - head.astype(jnp.float32)
        out[...] = jnp.where(third, tail, head.astype(jnp.float32)).astype(jnp.bfloat16)


class Rows:
    def __init__(self, lev, *pieces):
        self.lev = lev
        self.where = {}
        for buf, rows in pieces:
            for k, i in enumerate(rows):
                for f in range(2):
                    if isinstance(buf, tuple):
                        self.where[f, i] = (buf[f], k * lev)
                    else:
                        self.where[f, i] = (buf, (f * len(rows) + k) * lev)

    def read(self, f, i):
        buf, at = self.where[f, i]
        return buf[at : at + self.lev, :]

    def write(self, f, i, value):
        buf, at = self.where[f, i]
        buf[at : at + self.lev, :] = value


OWN = (0, 1, 2, 3)
OUTER = (-1, -2, -3, -4)
INNER = (7, 6, 5, 4)


def known(own, outer, inner):
    pieces = ((own, OWN), (outer, OUTER), (inner, INNER))
    return [piece for piece in pieces if piece[0] is not None]


def state_rows(own, outer, inner):
    lev = (own.shape[0] - 8) // 8
    return Rows(lev, *known(own, outer, inner))


class Factors:
    def __init__(self, own, outer, inner):
        self.end = own.shape[0] - 8
        self.lev = self.end // 8
        self.where = {}
        for buf, rows in known(own, outer, inner):
            for k, i in enumerate(rows):
                self.where[i] = (buf, k)

    def line(self, i, kind):
        buf, k = self.where[i]
        at = self.end + 4 * kind + k
        return jnp.broadcast_to(buf[at : at + 1, :], (8, buf.shape[1]))

    def keep(self, i):
        return self.line(i, 0)

    def drag(self, i):
        return self.line(i, 1)


def tiled(block, lev):
    return jnp.concatenate([block] * (lev // 8), axis=0)


def solve(matrix, first, second):
    both = jnp.concatenate([first, second], axis=1)
    head = both.astype(jnp.bfloat16)
    tail = (both - head.astype(jnp.float32)).astype(jnp.bfloat16)
    out = jnp.dot(
        matrix, jnp.concatenate([head, tail, head], axis=0), preferred_element_type=jnp.float32
    )
    half = first.shape[1]
    return out[:, :half], out[:, half:]


def beside(value):
    lev, width = value.shape
    step = 128
    lane = lax.broadcasted_iota(jnp.int32, (lev, step), 1)
    parts = [value[:, c : c + step] for c in range(0, width, step)]
    up = [pltpu.roll(part, 1, 1) for part in parts]
    down = [pltpu.roll(part, step - 1, 1) for part in parts]
    zero = jnp.zeros_like(up[0])
    sums = []
    for k in range(len(parts)):
        west = jnp.where(lane == 0, up[k - 1] if k > 0 else zero, up[k])
        east = jnp.where(lane == step - 1, down[k + 1] if k + 1 < len(parts) else zero, down[k])
        sums.append(west + east)
    return jnp.concatenate(sums, axis=1)


def state_row(i, side, x, factors, matrix, out):
    lev = x.lev
    keep, drag = factors.keep(i), factors.drag(i)
    near = tiled(diffusion * keep, lev)
    wind = side * x.read(0, i)
    parts = []
    for f in range(2):
        centre = x.read(f, i)
        up, down = x.read(f, i + 1), x.read(f, i - 1)
        own = tiled(keep * (0.6 - drag) if f == 0 else 0.6 * keep, lev)
        around = (up + down) + beside(centre) - wind * (up - down)
        parts.append(own * centre + near * around)
    for f, value in enumerate(solve(matrix, *parts)):
        out.write(f, i, value)


def tangent_row(i, side, d, x, factors, matrix, out, damp):
    lev = x.lev
    keep, drag = factors.keep(i), factors.drag(i)
    near = tiled(diffusion * keep, lev)
    wind = side * x.read(0, i)
    du = side * d.read(0, i)
    parts = []
    for f in range(2):
        centre = d.read(f, i)
        up, down = d.read(f, i + 1), d.read(f, i - 1)
        slope = x.read(f, i + 1) - x.read(f, i - 1)
        own = tiled(keep * (0.6 - drag) if f == 0 else 0.6 * keep, lev)
        around = (up + down) + beside(centre) - wind * (up - down) - du * slope
        parts.append(own * centre + near * around)
    for f, value in enumerate(solve(matrix, *parts)):
        out.write(f, i, value * tiled(keep, lev) if damp else value)


def adjoint_row(i, side, b, x, factors):
    lev = x.lev
    drag = factors.drag(i)
    more = 1.0 + side * x.read(0, i + 1)
    less = 1.0 - side * x.read(0, i - 1)
    parts = []
    sloped = 0.0
    for f in range(2):
        centre = b.read(f, i)
        sloped = sloped + centre * (x.read(f, i + 1) - x.read(f, i - 1))
        around = more * b.read(f, i + 1) + less * b.read(f, i - 1) + beside(centre)
        parts.append((centre, around))
    wind_part = tiled(0.6 - drag, lev) * parts[0][0] + diffusion * (parts[0][1] - side * sloped)
    heat_part = 0.6 * parts[1][0] + diffusion * parts[1][1]
    return wind_part, heat_part


def adjoint_solved(i, side, b, x, factors, matrix, out):
    keep = tiled(factors.keep(i), x.lev)
    for f, value in enumerate(solve(matrix, *adjoint_row(i, side, b, x, factors))):
        out.write(f, i, value * keep)


def span(first, last):
    return tuple(range(first, last))


def forward(side, state, start, factors, xs, moved, once, twice, ranges):
    for i in ranges[0]:
        state_row(i, side, state, factors, once, xs[0])
    for i in ranges[1]:
        state_row(i, side, xs[0], factors, once, xs[1])
    for i in ranges[2]:
        tangent_row(i, side, start, state, factors, once, moved[0], False)
    for i in ranges[3]:
        tangent_row(i, side, moved[0], xs[0], factors, once, moved[1], False)
    for i in ranges[4]:
        tangent_row(i, side, moved[1], xs[1], factors, twice, moved[2], True)


def inner_forward_kernel(
    side, own, inner, p_own, p_inner, once, twice,
    x1, x2, t1, t2, b2,
):
    state = state_rows(own, None, inner)
    lev = state.lev
    forward(
        side[0],
        state,
        Rows(lev, (p_own, OWN), (p_inner, INNER)),
        Factors(own, None, inner),
        (Rows(lev, (x1, span(1, 7))), Rows(lev, (x2, span(2, 6)))),
        (Rows(lev, (t1, span(1, 7))), Rows(lev, (t2, span(2, 6))), Rows(lev, (b2, span(3, 5)))),
        once[...],
        twice[...],
        (span(1, 7), span(2, 6), span(1, 7), span(2, 6), span(3, 5)),
    )


def forward_kernel(
    side, own, p_own, both_outer, x1_in, x2_in, t1_in, t2_in, b2_in, once, twice,
    outer_rows, x1, x2, b2,
    t1, t2,
):
    sign = side[0]
    size = own.shape[0]
    outer = both_outer.at[pl.ds(0, size)]
    p_outer = both_outer.at[pl.ds(size, p_own.shape[0])]
    state = state_rows(own, outer, None)
    factors = Factors(own, outer, None)
    lev = state.lev
    xs = (
        Rows(lev, (x1, span(-3, 1)), (x1_in, span(1, 7))),
        Rows(lev, (x2, span(-2, 2)), (x2_in, span(2, 6))),
    )
    moved = (
        Rows(lev, (t1, span(-3, 1)), (t1_in, span(1, 7))),
        Rows(lev, (t2, span(-2, 2)), (t2_in, span(2, 6))),
        Rows(lev, (b2, span(-1, 3)), (b2_in, span(3, 5))),
    )
    forward(
        sign,
        state,
        Rows(lev, (p_own, OWN), (p_outer, OUTER)),
        factors,
        xs,
        moved,
        once[...],
        twice[...],
        (span(-3, 1), span(-2, 2), span(-3, 1), span(-2, 2), span(-1, 3)),
    )
    out = Rows(lev, (outer_rows, (0, 1)))
    for i in (0, 1):
        adjoint_solved(i, sign, moved[2], xs[1], factors, once[...], out)


def inner_rows_kernel(side, own, x2, x2_in, b2, b2_in, once, inner_u, inner_t):
    factors = Factors(own, None, None)
    lev = factors.lev
    third = Rows(lev, (x2, span(-2, 2)), (x2_in, span(2, 6)))
    back = Rows(lev, (b2, span(-1, 3)), (b2_in, span(3, 5)))
    out = Rows(lev, ((inner_u, inner_t), (3, 2)))
    for i in (2, 3):
        adjoint_solved(i, side[0], back, third, factors, once[...], out)


def inner_backward_kernel(
    side, own, inner, x1, x1_in, outer_rows, inner_u, inner_t, b_u, b_t, once,
    b0, done,
):
    sign = side[0]
    state = state_rows(own, None, inner)
    factors = Factors(own, None, inner)
    lev = state.lev
    second = Rows(lev, (x1, span(-3, 1)), (x1_in, span(1, 7)))
    back = Rows(
        lev, (outer_rows, (0, 1)), ((inner_u, inner_t), (3, 2)), ((b_u, b_t), (4, 5))
    )
    last = Rows(lev, (b0, span(1, 5)))
    for i in span(1, 5):
        adjoint_solved(i, sign, back, second, factors, once[...], last)
    out = Rows(lev, (done, (2, 3)))
    for i in (2, 3):
        for f, value in enumerate(adjoint_row(i, sign, last, state, factors)):
            out.write(f, i, value)


def backward_kernel(
    side, own, both_outer, x1, x1_in, outer_rows, inner_u, inner_t, b_outer, b0_in, done, once,
    packed, field,
    b0, sems,
):
    sign = side[0]
    outer = both_outer.at[pl.ds(0, own.shape[0])]
    state = state_rows(own, outer, None)
    factors = Factors(own, outer, None)
    lev = state.lev
    second = Rows(lev, (x1, span(-3, 1)), (x1_in, span(1, 7)))
    back = Rows(
        lev, (outer_rows, (0, 1)), ((inner_u, inner_t), (3, 2)), (b_outer, (-1, -2))
    )
    last = Rows(lev, (b0, (-1, 0)), (b0_in, span(1, 5)))
    ready = Rows(lev, (done, (2, 3)))
    results = Rows(lev, (packed, OWN))
    copies = []

    def send(f, i):
        k = 4 * f + i
        row = jnp.where(sign < 0.0, 3 - i, i)
        copies.append(
            pltpu.make_async_copy(
                packed.at[pl.ds(k * lev, lev), :], field.at[:, f, row, :], sems.at[k]
            )
        )
        copies[-1].start()

    for i in (2, 3):
        for f in range(2):
            results.write(f, i, ready.read(f, i))
            send(f, i)
    for i in (-1, 0):
        adjoint_solved(i, sign, back, second, factors, once[...], last)
    for i in (0, 1):
        for f, value in enumerate(adjoint_row(i, sign, last, state, factors)):
            results.write(f, i, value)
            send(f, i)
    wait_all(copies)


def per_device(initial_state, perturbation, land_sea, relax_level, vertical_mix):
    lev, fields, rows, width = initial_state.shape
    tiles = lax.axis_size("tile")
    members = lax.axis_size("group")
    high = fields * rows * lev
    dma = pltpu.SemaphoreType.DMA
    side = (1 - 2 * (lax.axis_index("tile") & 1)).astype(jnp.float32)[None]
    across = [(i, i + 1) for i in range(1, tiles - 1, 2)]
    within = [(i, i + 1) for i in range(0, tiles, 2)]

    def swap(value, pairs):
        return lax.ppermute(value, "tile", pairs + [(j, i) for i, j in pairs])

    def buffer(n):
        return pltpu.VMEM((fields * n * lev, width), jnp.float32)

    def rows_of(n):
        return f32(fields * n * lev, width)

    both = run(
        pack_kernel,
        f32(2 * high + 2 * rows, width),
        [SMEM] + [ANY] * 4,
        ANY,
        [
            dma((2, fields * rows)),
            pltpu.VMEM((2, rows, width), jnp.int32),
            dma((2,)),
            pltpu.VMEM((2 * high + 2 * rows, width), jnp.float32),
            dma((2 * fields * rows + 1,)),
        ],
        2**20,
        60 * 2**20,
    )(side, initial_state, perturbation[0], land_sea, relax_level)
    both_outer = swap(both, across)
    state, start = run(
        split_kernel,
        (f32(high + 2 * rows, width), f32(high, width)),
        [ANY],
        (VMEM, VMEM),
        [dma((2,))],
        nbytes=2**18,
    )(both)
    state_inner = swap(state, within)
    start_inner = swap(start, within)

    weights = jax.ShapeDtypeStruct((lev, 3 * lev), jnp.bfloat16)
    once, twice = run(
        inverse_kernel,
        (weights, weights),
        [SMEM],
        (VMEM, VMEM),
        [pltpu.VMEM((lev, 3 * lev), jnp.float32)],
        nbytes=2**18,
    )(vertical_mix)

    x1_in, x2_in, t1, t2, b2 = run(
        inner_forward_kernel,
        (rows_of(6), rows_of(4), rows_of(6), rows_of(4), rows_of(2)),
        [SMEM] + [VMEM] * 6,
        (VMEM,) * 5,
        [],
        nbytes=2**18,
    )(side, state, state_inner, start, start_inner, once, twice)
    outer_rows, x1, x2, b2_outer = run(
        forward_kernel,
        (rows_of(2), rows_of(4), rows_of(4), rows_of(4)),
        [SMEM] + [VMEM] * 10,
        (VMEM,) * 4,
        [buffer(4), buffer(4)],
        nbytes=2**20,
    )(side, state, start, both_outer, x1_in, x2_in, t1, t2, b2, once, twice)

    b_outer = swap(outer_rows, across)
    half = f32(2 * lev, width)
    inner_u, inner_t = run(
        inner_rows_kernel,
        (half, half),
        [SMEM] + [VMEM] * 6,
        (VMEM, VMEM),
        [],
        nbytes=0,
    )(side, state, x2, x2_in, b2_outer, b2, once)
    b_u, b_t = swap(inner_u, within), swap(inner_t, within)
    b0, done = run(
        inner_backward_kernel,
        (rows_of(4), rows_of(2)),
        [SMEM] + [VMEM] * 10,
        (VMEM, VMEM),
        [],
        nbytes=0,
    )(side, state, state_inner, x1, x1_in, outer_rows, inner_u, inner_t, b_u, b_t, once)
    packed, field = run(
        backward_kernel,
        (f32(high, width), f32(lev, fields, rows, width)),
        [SMEM] + [VMEM] * 11,
        (VMEM, ANY),
        [buffer(2), dma((fields * rows,))],
        nbytes=2**20,
    )(
        side, state, both_outer, x1, x1_in, outer_rows, inner_u, inner_t, b_outer, b0, done, once
    )

    share = lax.all_to_all(
        packed.reshape(members, high // members, width), "group", 0, 0, tiled=True
    )
    products = lax.dot_general(
        share,
        share,
        (((1, 2), (1, 2)), ((), ())),
        precision=lax.Precision.HIGHEST,
        preferred_element_type=jnp.float32,
    )
    row = jnp.sum(lax.all_to_all(products, "group", 0, 0, tiled=True), axis=0)
    spread = jnp.broadcast_to(row[None], (tiles, members))
    row = jnp.sum(lax.all_to_all(spread, "tile", 0, 0, tiled=True), axis=0)
    gram = row[None] / (high * width * tiles)
    return (field[None], gram)


def solution(mesh):
    placed = (
        P(None, None, "tile", None),
        P("group", None, None, "tile", None),
        P("tile", None),
        P("tile", None),
        P(),
    )
    return jax.shard_map(
        per_device,
        mesh=mesh,
        in_specs=placed,
        out_specs=(P("group", None, None, "tile", None), P("group", None)),
        check_vma=False,
    )
```

```python
import jax
import jax.numpy as jnp
from jax import lax
from jax.experimental import pallas as pl
from jax.experimental.pallas import tpu as pltpu
from jax.sharding import PartitionSpec as P

advection = 0.2
diffusion = 0.1
drag_rate = 0.3
relaxation = 0.125

VMEM_LIMIT = 24 * 2**20
PAD = 16

ANY = pl.BlockSpec(memory_space=pl.ANY)
VMEM = pl.BlockSpec(memory_space=pltpu.VMEM)
SMEM = pl.BlockSpec(memory_space=pltpu.SMEM)


def run(kernel, out_shape, in_specs, out_specs, scratch, nbytes, limit=VMEM_LIMIT):
    return pl.pallas_call(
        kernel,
        out_shape=out_shape,
        in_specs=in_specs,
        out_specs=out_specs,
        scratch_shapes=scratch,
        compiler_params=pltpu.CompilerParams(vmem_limit_bytes=limit),
        cost_estimate=pl.CostEstimate(flops=0, bytes_accessed=nbytes, transcendentals=0),
    )


def f32(*shape):
    return jax.ShapeDtypeStruct(shape, jnp.float32)


def start_all(copies):
    for copy in copies:
        copy.start()


def wait_all(copies):
    for copy in copies:
        copy.wait()


def place_of(f, r, rows, flipped):
    return f * rows + jnp.where(flipped, rows - 1 - r, r)


def pack_rows(src, dst, sems, flipped, base):
    lev, fields, rows, _ = src.shape
    return [
        pltpu.make_async_copy(
            src.at[:, f, r, :],
            dst.at[pl.ds(pl.multiple_of(base + place_of(f, r, rows, flipped) * lev, 8), lev), :],
            sems.at[f * rows + r],
        )
        for f in range(fields)
        for r in range(rows)
    ]


def fill_lines(ints, out, flipped, end):
    rows = ints.shape[1]
    keep = 1.0 - relaxation * ints[0].astype(jnp.float32)
    drag = drag_rate * ints[1].astype(jnp.float32)
    for k, values in enumerate((keep, drag)):
        for r in range(rows):
            other = rows - 1 - r
            line = jnp.where(flipped, values[other : other + 1], values[r : r + 1])
            out[end + k * rows + r : end + k * rows + r + 1, :] = line


def pack_kernel(side, x, p, land, relax, out, sems, ints, more_sems, staged, out_sems):
    flipped = side[0] < 0.0
    lev, fields, rows, _ = x.shape
    high = fields * rows * lev
    loads = [
        pltpu.make_async_copy(src, ints.at[k], more_sems.at[k])
        for k, src in enumerate((relax, land))
    ]
    copies = pack_rows(x, staged, sems.at[0], flipped, 0)
    copies += pack_rows(p, staged, sems.at[1], flipped, high + 2 * rows)
    start_all(loads)
    start_all(copies)
    wait_all(loads)
    fill_lines(ints, staged, flipped, high)
    pieces = [
        pl.ds(pl.multiple_of(base + place_of(f, r, rows, flipped) * lev, 8), lev)
        for base in (0, high + 2 * rows)
        for f in range(fields)
        for r in range(rows)
    ]
    pieces.append(pl.ds(high, 2 * rows))
    outs = [
        pltpu.make_async_copy(staged.at[piece], out.at[piece], out_sems.at[k])
        for k, piece in enumerate(pieces)
    ]
    outs[-1].start()
    for copy, onward in zip(copies, outs):
        copy.wait()
        onward.start()
    wait_all(outs)


def split_kernel(both, state, start, sems):
    size = state.shape[0]
    copies = [
        pltpu.make_async_copy(both.at[pl.ds(0, size)], state, sems.at[0]),
        pltpu.make_async_copy(both.at[pl.ds(size, start.shape[0])], start, sems.at[1]),
    ]
    start_all(copies)
    wait_all(copies)


def inverse_kernel(mix, once, twice, solved):
    lev = mix.shape[0]
    wide = solved.shape[1]
    lane = lax.broadcasted_iota(jnp.int32, (1, wide), 1)
    unit = lane % lev
    ratio = []
    before = None
    inv = None
    for l in range(lev):
        rhs = jnp.where(unit == l, 1.0, 0.0).astype(jnp.float32)
        if l == 0:
            diag = jnp.full((1, wide), 1.0 + mix[0], jnp.float32)
        else:
            m = mix[l - 1]
            diag = (1.0 + mix[l] + m) - (m * m) * inv
            rhs = rhs + m * before
        inv = 1.0 / diag
        before = rhs * inv
        solved[l : l + 1, :] = before
        ratio.append(inv)
    for l in reversed(range(lev - 1)):
        before = solved[l : l + 1, :] + mix[l] * ratio[l] * before
        solved[l : l + 1, :] = before
    single = solved[...]
    double = jnp.dot(
        single[:, :lev],
        single,
        precision=lax.Precision.HIGHEST,
        preferred_element_type=jnp.float32,
    )
    third = lax.broadcasted_iota(jnp.int32, (lev, wide), 1) >= 2 * lev
    for matrix, out in ((single, once), (double, twice)):
        head = matrix.astype(jnp.bfloat16)
        tail = matrix - head.astype(jnp.float32)
        out[...] = jnp.where(third, tail, head.astype(jnp.float32)).astype(jnp.bfloat16)


class Rows:
    def __init__(self, lev, *pieces):
        self.lev = lev
        self.where = {}
        for buf, rows in pieces:
            for k, i in enumerate(rows):
                for f in range(2):
                    self.where[f, i] = (buf, (f * len(rows) + k) * lev)

    def read(self, f, i):
        buf, at = self.where[f, i]
        return buf[at : at + self.lev, :]

    def write(self, f, i, value):
        buf, at = self.where[f, i]
        buf[at : at + self.lev, :] = value


OWN = (0, 1, 2, 3)
OUTER = (-1, -2, -3, -4)
INNER = (7, 6, 5, 4)


def known(own, outer, inner):
    pieces = ((own, OWN), (outer, OUTER), (inner, INNER))
    return [piece for piece in pieces if piece[0] is not None]


def state_rows(own, outer, inner):
    lev = (own.shape[0] - 8) // 8
    return Rows(lev, *known(own, outer, inner))


class Factors:
    def __init__(self, own, outer, inner):
        self.end = own.shape[0] - 8
        self.lev = self.end // 8
        self.where = {}
        for buf, rows in known(own, outer, inner):
            for k, i in enumerate(rows):
                self.where[i] = (buf, k)

    def line(self, i, kind):
        buf, k = self.where[i]
        at = self.end + 4 * kind + k
        return jnp.broadcast_to(buf[at : at + 1, :], (8, buf.shape[1]))

    def keep(self, i):
        return self.line(i, 0)

    def drag(self, i):
        return self.line(i, 1)


def tiled(block, lev):
    return jnp.concatenate([block] * (lev // 8), axis=0)


def solve(matrix, first, second):
    both = jnp.concatenate([first, second], axis=1)
    head = both.astype(jnp.bfloat16)
    tail = (both - head.astype(jnp.float32)).astype(jnp.bfloat16)
    out = jnp.dot(
        matrix, jnp.concatenate([head, tail, head], axis=0), preferred_element_type=jnp.float32
    )
    half = first.shape[1]
    return out[:, :half], out[:, half:]


def beside(value):
    lev, width = value.shape
    step = 128
    lane = lax.broadcasted_iota(jnp.int32, (lev, step), 1)
    parts = [value[:, c : c + step] for c in range(0, width, step)]
    up = [pltpu.roll(part, 1, 1) for part in parts]
    down = [pltpu.roll(part, step - 1, 1) for part in parts]
    zero = jnp.zeros_like(up[0])
    sums = []
    for k in range(len(parts)):
        west = jnp.where(lane == 0, up[k - 1] if k > 0 else zero, up[k])
        east = jnp.where(lane == step - 1, down[k + 1] if k + 1 < len(parts) else zero, down[k])
        sums.append(west + east)
    return jnp.concatenate(sums, axis=1)


def state_row(i, side, x, factors, matrix, out):
    lev = x.lev
    keep, drag = factors.keep(i), factors.drag(i)
    near = tiled(diffusion * keep, lev)
    wind = side * x.read(0, i)
    parts = []
    for f in range(2):
        centre = x.read(f, i)
        up, down = x.read(f, i + 1), x.read(f, i - 1)
        own = tiled(keep * (0.6 - drag) if f == 0 else 0.6 * keep, lev)
        around = (up + down) + beside(centre) - wind * (up - down)
        parts.append(own * centre + near * around)
    for f, value in enumerate(solve(matrix, *parts)):
        out.write(f, i, value)


def tangent_row(i, side, d, x, factors, matrix, out, damp):
    lev = x.lev
    keep, drag = factors.keep(i), factors.drag(i)
    near = tiled(diffusion * keep, lev)
    wind = side * x.read(0, i)
    du = side * d.read(0, i)
    parts = []
    for f in range(2):
        centre = d.read(f, i)
        up, down = d.read(f, i + 1), d.read(f, i - 1)
        slope = x.read(f, i + 1) - x.read(f, i - 1)
        own = tiled(keep * (0.6 - drag) if f == 0 else 0.6 * keep, lev)
        around = (up + down) + beside(centre) - wind * (up - down) - du * slope
        parts.append(own * centre + near * around)
    for f, value in enumerate(solve(matrix, *parts)):
        out.write(f, i, value * tiled(keep, lev) if damp else value)


def adjoint_row(i, side, b, x, factors):
    lev = x.lev
    drag = factors.drag(i)
    more = 1.0 + side * x.read(0, i + 1)
    less = 1.0 - side * x.read(0, i - 1)
    parts = []
    sloped = 0.0
    for f in range(2):
        centre = b.read(f, i)
        sloped = sloped + centre * (x.read(f, i + 1) - x.read(f, i - 1))
        around = more * b.read(f, i + 1) + less * b.read(f, i - 1) + beside(centre)
        parts.append((centre, around))
    wind_part = tiled(0.6 - drag, lev) * parts[0][0] + diffusion * (parts[0][1] - side * sloped)
    heat_part = 0.6 * parts[1][0] + diffusion * parts[1][1]
    return wind_part, heat_part


def adjoint_solved(i, side, b, x, factors, matrix, out):
    keep = tiled(factors.keep(i), x.lev)
    for f, value in enumerate(solve(matrix, *adjoint_row(i, side, b, x, factors))):
        out.write(f, i, value * keep)


def span(first, last):
    return tuple(range(first, last))


def forward(side, state, start, factors, xs, moved, once, twice, ranges):
    for i in ranges[0]:
        state_row(i, side, state, factors, once, xs[0])
    for i in ranges[1]:
        state_row(i, side, xs[0], factors, once, xs[1])
    for i in ranges[2]:
        tangent_row(i, side, start, state, factors, once, moved[0], False)
    for i in ranges[3]:
        tangent_row(i, side, moved[0], xs[0], factors, once, moved[1], False)
    for i in ranges[4]:
        tangent_row(i, side, moved[1], xs[1], factors, twice, moved[2], True)


def inner_forward_kernel(
    side, own, inner, p_own, p_inner, once, twice,
    x1, x2, t1, t2, b2,
):
    state = state_rows(own, None, inner)
    lev = state.lev
    forward(
        side[0],
        state,
        Rows(lev, (p_own, OWN), (p_inner, INNER)),
        Factors(own, None, inner),
        (Rows(lev, (x1, span(1, 7))), Rows(lev, (x2, span(2, 6)))),
        (Rows(lev, (t1, span(1, 7))), Rows(lev, (t2, span(2, 6))), Rows(lev, (b2, span(3, 5)))),
        once[...],
        twice[...],
        (span(1, 7), span(2, 6), span(1, 7), span(2, 6), span(3, 5)),
    )


def forward_kernel(
    side, own, p_own, both_outer, x1_in, x2_in, t1_in, t2_in, b2_in, once, twice,
    outer_rows, x1, x2, b2,
    t1, t2,
):
    sign = side[0]
    size = own.shape[0]
    outer = both_outer.at[pl.ds(0, size)]
    p_outer = both_outer.at[pl.ds(size, p_own.shape[0])]
    state = state_rows(own, outer, None)
    factors = Factors(own, outer, None)
    lev = state.lev
    xs = (
        Rows(lev, (x1, span(-3, 1)), (x1_in, span(1, 7))),
        Rows(lev, (x2, span(-2, 2)), (x2_in, span(2, 6))),
    )
    moved = (
        Rows(lev, (t1, span(-3, 1)), (t1_in, span(1, 7))),
        Rows(lev, (t2, span(-2, 2)), (t2_in, span(2, 6))),
        Rows(lev, (b2, span(-1, 3)), (b2_in, span(3, 5))),
    )
    forward(
        sign,
        state,
        Rows(lev, (p_own, OWN), (p_outer, OUTER)),
        factors,
        xs,
        moved,
        once[...],
        twice[...],
        (span(-3, 1), span(-2, 2), span(-3, 1), span(-2, 2), span(-1, 3)),
    )
    out = Rows(lev, (outer_rows, (0, 1)))
    outer_rows[outer_rows.shape[0] - PAD :, :] = jnp.zeros((PAD, own.shape[1]), jnp.float32)
    for i in (0, 1):
        adjoint_solved(i, sign, moved[2], xs[1], factors, once[...], out)


def inner_rows_kernel(side, own, x2, x2_in, b2, b2_in, once, inner_rows):
    factors = Factors(own, None, None)
    lev = factors.lev
    third = Rows(lev, (x2, span(-2, 2)), (x2_in, span(2, 6)))
    back = Rows(lev, (b2, span(-1, 3)), (b2_in, span(3, 5)))
    out = Rows(lev, (inner_rows, (3, 2)))
    for i in (2, 3):
        adjoint_solved(i, side[0], back, third, factors, once[...], out)


def inner_backward_kernel(
    side, own, inner, x1, x1_in, outer_rows, inner_rows, b_inner, once,
    b0, done,
):
    sign = side[0]
    state = state_rows(own, None, inner)
    factors = Factors(own, None, inner)
    lev = state.lev
    second = Rows(lev, (x1, span(-3, 1)), (x1_in, span(1, 7)))
    back = Rows(lev, (outer_rows, (0, 1)), (inner_rows, (3, 2)), (b_inner, (4, 5)))
    last = Rows(lev, (b0, span(1, 5)))
    for i in span(1, 5):
        adjoint_solved(i, sign, back, second, factors, once[...], last)
    out = Rows(lev, (done, (2, 3)))
    for i in (2, 3):
        for f, value in enumerate(adjoint_row(i, sign, last, state, factors)):
            out.write(f, i, value)


def backward_kernel(
    side, own, both_outer, x1, x1_in, outer_rows, inner_rows, b_outer, b0_in, done, once,
    packed, field,
    b0, sems,
):
    sign = side[0]
    outer = both_outer.at[pl.ds(0, own.shape[0])]
    state = state_rows(own, outer, None)
    factors = Factors(own, outer, None)
    lev = state.lev
    second = Rows(lev, (x1, span(-3, 1)), (x1_in, span(1, 7)))
    back = Rows(lev, (outer_rows, (0, 1)), (inner_rows, (3, 2)), (b_outer, (-1, -2)))
    last = Rows(lev, (b0, (-1, 0)), (b0_in, span(1, 5)))
    ready = Rows(lev, (done, (2, 3)))
    results = Rows(lev, (packed, OWN))
    copies = []

    def send(f, i):
        k = 4 * f + i
        row = jnp.where(sign < 0.0, 3 - i, i)
        copies.append(
            pltpu.make_async_copy(
                packed.at[pl.ds(k * lev, lev), :], field.at[:, f, row, :], sems.at[k]
            )
        )
        copies[-1].start()

    for i in (2, 3):
        for f in range(2):
            results.write(f, i, ready.read(f, i))
            send(f, i)
    for i in (-1, 0):
        adjoint_solved(i, sign, back, second, factors, once[...], last)
    for i in (0, 1):
        for f, value in enumerate(adjoint_row(i, sign, last, state, factors)):
            results.write(f, i, value)
            send(f, i)
    wait_all(copies)


def per_device(initial_state, perturbation, land_sea, relax_level, vertical_mix):
    lev, fields, rows, width = initial_state.shape
    tiles = lax.axis_size("tile")
    members = lax.axis_size("group")
    high = fields * rows * lev
    dma = pltpu.SemaphoreType.DMA
    side = (1 - 2 * (lax.axis_index("tile") & 1)).astype(jnp.float32)[None]
    across = [(i, i + 1) for i in range(1, tiles - 1, 2)]
    within = [(i, i + 1) for i in range(0, tiles, 2)]

    def swap(value, pairs):
        return lax.ppermute(value, "tile", pairs + [(j, i) for i, j in pairs])

    def buffer(n):
        return pltpu.VMEM((fields * n * lev, width), jnp.float32)

    def rows_of(n):
        return f32(fields * n * lev, width)

    both = run(
        pack_kernel,
        f32(2 * high + 2 * rows, width),
        [SMEM] + [ANY] * 4,
        ANY,
        [
            dma((2, fields * rows)),
            pltpu.VMEM((2, rows, width), jnp.int32),
            dma((2,)),
            pltpu.VMEM((2 * high + 2 * rows, width), jnp.float32),
            dma((2 * fields * rows + 1,)),
        ],
        2**20,
        60 * 2**20,
    )(side, initial_state, perturbation[0], land_sea, relax_level)
    both_outer = swap(both, across)
    state, start = run(
        split_kernel,
        (f32(high + 2 * rows, width), f32(high, width)),
        [ANY],
        (VMEM, VMEM),
        [dma((2,))],
        nbytes=2**18,
    )(both)
    state_inner = swap(state, within)
    start_inner = swap(start, within)

    weights = jax.ShapeDtypeStruct((lev, 3 * lev), jnp.bfloat16)
    once, twice = run(
        inverse_kernel,
        (weights, weights),
        [SMEM],
        (VMEM, VMEM),
        [pltpu.VMEM((lev, 3 * lev), jnp.float32)],
        nbytes=2**18,
    )(vertical_mix)

    x1_in, x2_in, t1, t2, b2 = run(
        inner_forward_kernel,
        (rows_of(6), rows_of(4), rows_of(6), rows_of(4), rows_of(2)),
        [SMEM] + [VMEM] * 6,
        (VMEM,) * 5,
        [],
        nbytes=2**18,
    )(side, state, state_inner, start, start_inner, once, twice)
    outer_shape = f32(fields * 2 * lev + PAD, width)
    outer_rows, x1, x2, b2_outer = run(
        forward_kernel,
        (outer_shape, rows_of(4), rows_of(4), rows_of(4)),
        [SMEM] + [VMEM] * 10,
        (VMEM,) * 4,
        [buffer(4), buffer(4)],
        nbytes=2**20,
    )(side, state, start, both_outer, x1_in, x2_in, t1, t2, b2, once, twice)

    b_outer = swap(outer_rows, across)
    inner_rows = run(
        inner_rows_kernel,
        rows_of(2),
        [SMEM] + [VMEM] * 6,
        VMEM,
        [],
        nbytes=0,
    )(side, state, x2, x2_in, b2_outer, b2, once)
    b_inner = swap(inner_rows, within)
    b0, done = run(
        inner_backward_kernel,
        (rows_of(4), rows_of(2)),
        [SMEM] + [VMEM] * 8,
        (VMEM, VMEM),
        [],
        nbytes=0,
    )(side, state, state_inner, x1, x1_in, outer_rows, inner_rows, b_inner, once)
    packed, field = run(
        backward_kernel,
        (f32(high, width), f32(lev, fields, rows, width)),
        [SMEM] + [VMEM] * 10,
        (VMEM, ANY),
        [buffer(2), dma((fields * rows,))],
        nbytes=2**20,
    )(
        side, state, both_outer, x1, x1_in, outer_rows, inner_rows, b_outer, b0, done, once
    )

    share = lax.all_to_all(
        packed.reshape(members, high // members, width), "group", 0, 0, tiled=True
    )
    products = lax.dot_general(
        share,
        share,
        (((1, 2), (1, 2)), ((), ())),
        precision=lax.Precision.HIGH,
        preferred_element_type=jnp.float32,
    ) * (1.0 / (high * width * tiles))
    row = jnp.sum(lax.all_to_all(products, "group", 0, 0, tiled=True), axis=0)
    spread = jnp.broadcast_to(row[None], (tiles, members))
    row = jnp.sum(lax.all_to_all(spread, "tile", 0, 0, tiled=True), axis=0)
    return (field[None], row[None])


def solution(mesh):
    placed = (
        P(None, None, "tile", None),
        P("group", None, None, "tile", None),
        P("tile", None),
        P("tile", None),
        P(),
    )
    return jax.shard_map(
        per_device,
        mesh=mesh,
        in_specs=placed,
        out_specs=(P("group", None, None, "tile", None), P("group", None)),
        check_vma=False,
    )
```

```python
import jax
import jax.numpy as jnp
from jax import lax
from jax.experimental import pallas as pl
from jax.experimental.pallas import tpu as pltpu
from jax.sharding import PartitionSpec as P

advection = 0.2
diffusion = 0.1
drag_rate = 0.3
relaxation = 0.125

VMEM_LIMIT = 24 * 2**20
PAD = 8

ANY = pl.BlockSpec(memory_space=pl.ANY)
VMEM = pl.BlockSpec(memory_space=pltpu.VMEM)
SMEM = pl.BlockSpec(memory_space=pltpu.SMEM)


def run(kernel, out_shape, in_specs, out_specs, scratch, nbytes, limit=VMEM_LIMIT):
    return pl.pallas_call(
        kernel,
        out_shape=out_shape,
        in_specs=in_specs,
        out_specs=out_specs,
        scratch_shapes=scratch,
        compiler_params=pltpu.CompilerParams(vmem_limit_bytes=limit),
        cost_estimate=pl.CostEstimate(flops=0, bytes_accessed=nbytes, transcendentals=0),
    )


def f32(*shape):
    return jax.ShapeDtypeStruct(shape, jnp.float32)


def start_all(copies):
    for copy in copies:
        copy.start()


def wait_all(copies):
    for copy in copies:
        copy.wait()


def place_of(f, r, rows, flipped):
    return f * rows + jnp.where(flipped, rows - 1 - r, r)


def pack_rows(src, dst, sems, flipped, base):
    lev, fields, rows, _ = src.shape
    return [
        pltpu.make_async_copy(
            src.at[:, f, r, :],
            dst.at[pl.ds(pl.multiple_of(base + place_of(f, r, rows, flipped) * lev, 8), lev), :],
            sems.at[f * rows + r],
        )
        for f in range(fields)
        for r in range(rows)
    ]


def fill_lines(ints, out, flipped, end):
    rows = ints.shape[1]
    keep = 1.0 - relaxation * ints[0].astype(jnp.float32)
    drag = drag_rate * ints[1].astype(jnp.float32)
    for k, values in enumerate((keep, drag)):
        for r in range(rows):
            other = rows - 1 - r
            line = jnp.where(flipped, values[other : other + 1], values[r : r + 1])
            out[end + k * rows + r : end + k * rows + r + 1, :] = line


def pack_kernel(side, x, p, land, relax, out, sems, ints, more_sems, staged, out_sems):
    flipped = side[0] < 0.0
    lev, fields, rows, _ = x.shape
    high = fields * rows * lev
    loads = [
        pltpu.make_async_copy(src, ints.at[k], more_sems.at[k])
        for k, src in enumerate((relax, land))
    ]
    copies = pack_rows(x, staged, sems.at[0], flipped, 0)
    copies += pack_rows(p, staged, sems.at[1], flipped, high + 2 * rows)
    start_all(loads)
    start_all(copies)
    wait_all(loads)
    fill_lines(ints, staged, flipped, high)
    pieces = [
        pl.ds(pl.multiple_of(base + place_of(f, r, rows, flipped) * lev, 8), lev)
        for base in (0, high + 2 * rows)
        for f in range(fields)
        for r in range(rows)
    ]
    pieces.append(pl.ds(high, 2 * rows))
    outs = [
        pltpu.make_async_copy(staged.at[piece], out.at[piece], out_sems.at[k])
        for k, piece in enumerate(pieces)
    ]
    outs[-1].start()
    for copy, onward in zip(copies, outs):
        copy.wait()
        onward.start()
    wait_all(outs)


def split_kernel(both, state, start, sems):
    size = state.shape[0]
    copies = [
        pltpu.make_async_copy(both.at[pl.ds(0, size)], state, sems.at[0]),
        pltpu.make_async_copy(both.at[pl.ds(size, start.shape[0])], start, sems.at[1]),
    ]
    start_all(copies)
    wait_all(copies)


def inverse_kernel(mix, once, twice, solved):
    lev = mix.shape[0]
    wide = solved.shape[1]
    lane = lax.broadcasted_iota(jnp.int32, (1, wide), 1)
    unit = lane % lev
    ratio = []
    before = None
    inv = None
    for l in range(lev):
        rhs = jnp.where(unit == l, 1.0, 0.0).astype(jnp.float32)
        if l == 0:
            diag = jnp.full((1, wide), 1.0 + mix[0], jnp.float32)
        else:
            m = mix[l - 1]
            diag = (1.0 + mix[l] + m) - (m * m) * inv
            rhs = rhs + m * before
        inv = 1.0 / diag
        before = rhs * inv
        solved[l : l + 1, :] = before
        ratio.append(inv)
    for l in reversed(range(lev - 1)):
        before = solved[l : l + 1, :] + mix[l] * ratio[l] * before
        solved[l : l + 1, :] = before
    single = solved[...]
    double = jnp.dot(
        single[:, :lev],
        single,
        precision=lax.Precision.HIGHEST,
        preferred_element_type=jnp.float32,
    )
    third = lax.broadcasted_iota(jnp.int32, (lev, wide), 1) >= 2 * lev
    for matrix, out in ((single, once), (double, twice)):
        head = matrix.astype(jnp.bfloat16)
        tail = matrix - head.astype(jnp.float32)
        out[...] = jnp.where(third, tail, head.astype(jnp.float32)).astype(jnp.bfloat16)


class Rows:
    def __init__(self, lev, *pieces):
        self.lev = lev
        self.where = {}
        for buf, rows in pieces:
            for k, i in enumerate(rows):
                for f in range(2):
                    self.where[f, i] = (buf, (f * len(rows) + k) * lev)

    def read(self, f, i):
        buf, at = self.where[f, i]
        return buf[at : at + self.lev, :]

    def write(self, f, i, value):
        buf, at = self.where[f, i]
        buf[at : at + self.lev, :] = value


OWN = (0, 1, 2, 3)
OUTER = (-1, -2, -3, -4)
INNER = (7, 6, 5, 4)


def known(own, outer, inner):
    pieces = ((own, OWN), (outer, OUTER), (inner, INNER))
    return [piece for piece in pieces if piece[0] is not None]


def state_rows(own, outer, inner):
    lev = (own.shape[0] - 8) // 8
    return Rows(lev, *known(own, outer, inner))


class Factors:
    def __init__(self, own, outer, inner):
        self.end = own.shape[0] - 8
        self.lev = self.end // 8
        self.where = {}
        for buf, rows in known(own, outer, inner):
            for k, i in enumerate(rows):
                self.where[i] = (buf, k)

    def line(self, i, kind):
        buf, k = self.where[i]
        at = self.end + 4 * kind + k
        return jnp.broadcast_to(buf[at : at + 1, :], (8, buf.shape[1]))

    def keep(self, i):
        return self.line(i, 0)

    def drag(self, i):
        return self.line(i, 1)


def tiled(block, lev):
    return jnp.concatenate([block] * (lev // 8), axis=0)


def solve(matrix, first, second):
    both = jnp.concatenate([first, second], axis=1)
    head = both.astype(jnp.bfloat16)
    tail = (both - head.astype(jnp.float32)).astype(jnp.bfloat16)
    out = jnp.dot(
        matrix, jnp.concatenate([head, tail, head], axis=0), preferred_element_type=jnp.float32
    )
    half = first.shape[1]
    return out[:, :half], out[:, half:]


def beside(value):
    lev, width = value.shape
    step = 128
    lane = lax.broadcasted_iota(jnp.int32, (lev, step), 1)
    parts = [value[:, c : c + step] for c in range(0, width, step)]
    up = [pltpu.roll(part, 1, 1) for part in parts]
    down = [pltpu.roll(part, step - 1, 1) for part in parts]
    zero = jnp.zeros_like(up[0])
    sums = []
    for k in range(len(parts)):
        west = jnp.where(lane == 0, up[k - 1] if k > 0 else zero, up[k])
        east = jnp.where(lane == step - 1, down[k + 1] if k + 1 < len(parts) else zero, down[k])
        sums.append(west + east)
    return jnp.concatenate(sums, axis=1)


def state_row(i, side, x, factors, matrix, out):
    lev = x.lev
    keep, drag = factors.keep(i), factors.drag(i)
    near = tiled(diffusion * keep, lev)
    wind = side * x.read(0, i)
    parts = []
    for f in range(2):
        centre = x.read(f, i)
        up, down = x.read(f, i + 1), x.read(f, i - 1)
        own = tiled(keep * (0.6 - drag) if f == 0 else 0.6 * keep, lev)
        around = (up + down) + beside(centre) - wind * (up - down)
        parts.append(own * centre + near * around)
    for f, value in enumerate(solve(matrix, *parts)):
        out.write(f, i, value)


def tangent_row(i, side, d, x, factors, matrix, out, damp):
    lev = x.lev
    keep, drag = factors.keep(i), factors.drag(i)
    near = tiled(diffusion * keep, lev)
    wind = x.read(0, i)
    du = d.read(0, i)
    signed = tiled((diffusion * side) * keep, lev)
    parts = []
    for f in range(2):
        centre = d.read(f, i)
        up, down = d.read(f, i + 1), d.read(f, i - 1)
        slope = x.read(f, i + 1) - x.read(f, i - 1)
        own = tiled(keep * (0.6 - drag) if f == 0 else 0.6 * keep, lev)
        moved = wind * (up - down) + du * slope
        parts.append(own * centre + near * ((up + down) + beside(centre)) - signed * moved)
    for f, value in enumerate(solve(matrix, *parts)):
        out.write(f, i, value * tiled(keep, lev) if damp else value)


def adjoint_row(i, side, b, x, factors):
    lev = x.lev
    drag = factors.drag(i)
    more = 1.0 + side * x.read(0, i + 1)
    less = 1.0 - side * x.read(0, i - 1)
    parts = []
    sloped = 0.0
    for f in range(2):
        centre = b.read(f, i)
        sloped = sloped + centre * (x.read(f, i + 1) - x.read(f, i - 1))
        around = more * b.read(f, i + 1) + less * b.read(f, i - 1) + beside(centre)
        parts.append((centre, around))
    wind_part = tiled(0.6 - drag, lev) * parts[0][0] + diffusion * (parts[0][1] - side * sloped)
    heat_part = 0.6 * parts[1][0] + diffusion * parts[1][1]
    return wind_part, heat_part


def adjoint_solved(i, side, b, x, factors, matrix, out):
    keep = tiled(factors.keep(i), x.lev)
    for f, value in enumerate(solve(matrix, *adjoint_row(i, side, b, x, factors))):
        out.write(f, i, value * keep)


def span(first, last):
    return tuple(range(first, last))


def forward(side, state, start, factors, xs, moved, once, twice, ranges):
    for i, j in zip(ranges[0], ranges[2]):
        state_row(i, side, state, factors, once, xs[0])
        tangent_row(j, side, start, state, factors, once, moved[0], False)
    for i, j in zip(ranges[1], ranges[3]):
        state_row(i, side, xs[0], factors, once, xs[1])
        tangent_row(j, side, moved[0], xs[0], factors, once, moved[1], False)
    for i in ranges[4]:
        tangent_row(i, side, moved[1], xs[1], factors, twice, moved[2], True)


def inner_forward_kernel(
    side, own, inner, p_own, p_inner, once, twice,
    x1, x2, t1, t2, b2,
):
    state = state_rows(own, None, inner)
    lev = state.lev
    forward(
        side[0],
        state,
        Rows(lev, (p_own, OWN), (p_inner, INNER)),
        Factors(own, None, inner),
        (Rows(lev, (x1, span(1, 7))), Rows(lev, (x2, span(2, 6)))),
        (Rows(lev, (t1, span(1, 7))), Rows(lev, (t2, span(2, 6))), Rows(lev, (b2, span(3, 5)))),
        once[...],
        twice[...],
        (span(1, 7), span(2, 6), span(1, 7), span(2, 6), span(3, 5)),
    )


def forward_kernel(
    side, own, p_own, both_outer, x1_in, x2_in, t1_in, t2_in, b2_in, once, twice,
    outer_rows, x1, x2, b2,
    t1, t2,
):
    sign = side[0]
    size = own.shape[0]
    outer = both_outer.at[pl.ds(0, size)]
    p_outer = both_outer.at[pl.ds(size, p_own.shape[0])]
    state = state_rows(own, outer, None)
    factors = Factors(own, outer, None)
    lev = state.lev
    xs = (
        Rows(lev, (x1, span(-3, 1)), (x1_in, span(1, 7))),
        Rows(lev, (x2, span(-2, 2)), (x2_in, span(2, 6))),
    )
    moved = (
        Rows(lev, (t1, span(-3, 1)), (t1_in, span(1, 7))),
        Rows(lev, (t2, span(-2, 2)), (t2_in, span(2, 6))),
        Rows(lev, (b2, span(-1, 3)), (b2_in, span(3, 5))),
    )
    forward(
        sign,
        state,
        Rows(lev, (p_own, OWN), (p_outer, OUTER)),
        factors,
        xs,
        moved,
        once[...],
        twice[...],
        (span(-3, 1), span(-2, 2), span(-3, 1), span(-2, 2), span(-1, 3)),
    )
    out = Rows(lev, (outer_rows, (0, 1)))
    outer_rows[outer_rows.shape[0] - PAD :, :] = jnp.zeros((PAD, own.shape[1]), jnp.float32)
    for i in (0, 1):
        adjoint_solved(i, sign, moved[2], xs[1], factors, once[...], out)


def inner_rows_kernel(side, own, x2, x2_in, b2, b2_in, once, inner_rows):
    factors = Factors(own, None, None)
    lev = factors.lev
    third = Rows(lev, (x2, span(-2, 2)), (x2_in, span(2, 6)))
    back = Rows(lev, (b2, span(-1, 3)), (b2_in, span(3, 5)))
    out = Rows(lev, (inner_rows, (3, 2)))
    for i in (2, 3):
        adjoint_solved(i, side[0], back, third, factors, once[...], out)


def inner_backward_kernel(
    side, own, inner, x1, x1_in, outer_rows, inner_rows, b_inner, once,
    b0, done,
):
    sign = side[0]
    state = state_rows(own, None, inner)
    factors = Factors(own, None, inner)
    lev = state.lev
    second = Rows(lev, (x1, span(-3, 1)), (x1_in, span(1, 7)))
    back = Rows(lev, (outer_rows, (0, 1)), (inner_rows, (3, 2)), (b_inner, (4, 5)))
    last = Rows(lev, (b0, span(1, 5)))
    for i in span(1, 5):
        adjoint_solved(i, sign, back, second, factors, once[...], last)
    out = Rows(lev, (done, (2, 3)))
    for i in (2, 3):
        for f, value in enumerate(adjoint_row(i, sign, last, state, factors)):
            out.write(f, i, value)


def backward_kernel(
    side, own, both_outer, x1, x1_in, outer_rows, inner_rows, b_outer, b0_in, done, once,
    packed, field,
    b0, sems,
):
    sign = side[0]
    outer = both_outer.at[pl.ds(0, own.shape[0])]
    state = state_rows(own, outer, None)
    factors = Factors(own, outer, None)
    lev = state.lev
    second = Rows(lev, (x1, span(-3, 1)), (x1_in, span(1, 7)))
    back = Rows(lev, (outer_rows, (0, 1)), (inner_rows, (3, 2)), (b_outer, (-1, -2)))
    last = Rows(lev, (b0, (-1, 0)), (b0_in, span(1, 5)))
    ready = Rows(lev, (done, (2, 3)))
    results = Rows(lev, (packed, OWN))
    copies = []

    def send(f, i):
        k = 4 * f + i
        row = jnp.where(sign < 0.0, 3 - i, i)
        copies.append(
            pltpu.make_async_copy(
                packed.at[pl.ds(k * lev, lev), :], field.at[:, f, row, :], sems.at[k]
            )
        )
        copies[-1].start()

    for i in (2, 3):
        for f in range(2):
            results.write(f, i, ready.read(f, i))
            send(f, i)
    for i in (-1, 0):
        adjoint_solved(i, sign, back, second, factors, once[...], last)
    for i in (0, 1):
        for f, value in enumerate(adjoint_row(i, sign, last, state, factors)):
            results.write(f, i, value)
            send(f, i)
    wait_all(copies)


def per_device(initial_state, perturbation, land_sea, relax_level, vertical_mix):
    lev, fields, rows, width = initial_state.shape
    tiles = lax.axis_size("tile")
    members = lax.axis_size("group")
    high = fields * rows * lev
    dma = pltpu.SemaphoreType.DMA
    side = (1 - 2 * (lax.axis_index("tile") & 1)).astype(jnp.float32)[None]
    across = [(i, i + 1) for i in range(1, tiles - 1, 2)]
    within = [(i, i + 1) for i in range(0, tiles, 2)]

    def swap(value, pairs):
        return lax.ppermute(value, "tile", pairs + [(j, i) for i, j in pairs])

    def buffer(n):
        return pltpu.VMEM((fields * n * lev, width), jnp.float32)

    def rows_of(n):
        return f32(fields * n * lev, width)

    both = run(
        pack_kernel,
        f32(2 * high + 2 * rows, width),
        [SMEM] + [ANY] * 4,
        ANY,
        [
            dma((2, fields * rows)),
            pltpu.VMEM((2, rows, width), jnp.int32),
            dma((2,)),
            pltpu.VMEM((2 * high + 2 * rows, width), jnp.float32),
            dma((2 * fields * rows + 1,)),
        ],
        2**20,
        60 * 2**20,
    )(side, initial_state, perturbation[0], land_sea, relax_level)
    both_outer = swap(both, across)
    state, start = run(
        split_kernel,
        (f32(high + 2 * rows, width), f32(high, width)),
        [ANY],
        (VMEM, VMEM),
        [dma((2,))],
        nbytes=2**18,
    )(both)
    state_inner = swap(state, within)
    start_inner = swap(start, within)

    weights = jax.ShapeDtypeStruct((lev, 3 * lev), jnp.bfloat16)
    once, twice = run(
        inverse_kernel,
        (weights, weights),
        [SMEM],
        (VMEM, VMEM),
        [pltpu.VMEM((lev, 3 * lev), jnp.float32)],
        nbytes=2**18,
    )(vertical_mix)

    x1_in, x2_in, t1, t2, b2 = run(
        inner_forward_kernel,
        (rows_of(6), rows_of(4), rows_of(6), rows_of(4), rows_of(2)),
        [SMEM] + [VMEM] * 6,
        (VMEM,) * 5,
        [],
        nbytes=2**18,
    )(side, state, state_inner, start, start_inner, once, twice)
    outer_shape = f32(fields * 2 * lev + PAD, width)
    outer_rows, x1, x2, b2_outer = run(
        forward_kernel,
        (outer_shape, rows_of(4), rows_of(4), rows_of(4)),
        [SMEM] + [VMEM] * 10,
        (VMEM,) * 4,
        [buffer(4), buffer(4)],
        nbytes=2**20,
    )(side, state, start, both_outer, x1_in, x2_in, t1, t2, b2, once, twice)

    b_outer = swap(outer_rows, across)
    inner_rows = run(
        inner_rows_kernel,
        rows_of(2),
        [SMEM] + [VMEM] * 6,
        VMEM,
        [],
        nbytes=0,
    )(side, state, x2, x2_in, b2_outer, b2, once)
    b_inner = swap(inner_rows, within)
    b0, done = run(
        inner_backward_kernel,
        (rows_of(4), rows_of(2)),
        [SMEM] + [VMEM] * 8,
        (VMEM, VMEM),
        [],
        nbytes=0,
    )(side, state, state_inner, x1, x1_in, outer_rows, inner_rows, b_inner, once)
    packed, field = run(
        backward_kernel,
        (f32(high, width), f32(lev, fields, rows, width)),
        [SMEM] + [VMEM] * 10,
        (VMEM, ANY),
        [buffer(2), dma((fields * rows,))],
        nbytes=2**20,
    )(
        side, state, both_outer, x1, x1_in, outer_rows, inner_rows, b_outer, b0, done, once
    )

    share = lax.all_to_all(
        packed.reshape(members, high // members, width), "group", 0, 0, tiled=True
    )
    products = lax.dot_general(
        share,
        share,
        (((1, 2), (1, 2)), ((), ())),
        precision=lax.Precision.HIGH,
        preferred_element_type=jnp.float32,
    ) * (1.0 / (high * width * tiles))
    row = jnp.sum(lax.all_to_all(products, "group", 0, 0, tiled=True), axis=0)
    spread = jnp.broadcast_to(row[None], (tiles, members))
    row = jnp.sum(lax.all_to_all(spread, "tile", 0, 0, tiled=True), axis=0)
    return (field[None], row[None])


def solution(mesh):
    placed = (
        P(None, None, "tile", None),
        P("group", None, None, "tile", None),
        P("tile", None),
        P("tile", None),
        P(),
    )
    return jax.shard_map(
        per_device,
        mesh=mesh,
        in_specs=placed,
        out_specs=(P("group", None, None, "tile", None), P("group", None)),
        check_vma=False,
    )
```
